256 devices in a mesh: dp: 4 (over x_hi, core), row: 8 (over z), col: 8 (over x_lo, y).
Axes of the slice: x: 4 (x_hi: 2, x_lo: 2; x = x_hi * 2 + x_lo), y: 4, z: 8, core: 2. Of those that a mesh axis runs over, the one named last changes fastest.
Arguments:
- pair_rep: bfloat16 [4096, 1024, 128], P(('dp', 'row'), 'col'), parts along dimension 0, may hold values from -6 to 6
- pair_mask: int32 [4096, 1024], P(('dp', 'row'), 'col'), parts along dimension 0, may hold values from 0 to 1, as said below
- w_left_gate: bfloat16 [128, 128], replicated, may hold values from -0.5 to 0.5
- w_left_proj: bfloat16 [128, 128], replicated, may hold values from -0.5 to 0.5
- w_right_gate: bfloat16 [128, 128], replicated, may hold values from -0.5 to 0.5
- w_right_proj: bfloat16 [128, 128], replicated, may hold values from -0.5 to 0.5
- w_gate: bfloat16 [128, 128], replicated, may hold values from -0.5 to 0.5
- w_out: bfloat16 [128, 128], replicated, may hold values from -0.5 to 0.5
Outputs:
- update: bfloat16 [4096, 1024, 128], P(('dp', 'row'), 'col'), parts along dimension 0
The draws below stay inside these ranges and needn't reach their ends.
There are 4 independent parts, one for each index of `dp`. The reference program is written for one: setup_inputs(seed, part) draws one part's arguments, and reference() takes and returns one part's arrays. A program takes and returns all parts, laid end to end along the dimension named above; an argument that names none is the same for every part. Nothing has to cross between parts.
Inputs may be any that keep to these rules, and one draw needn't show every extreme that they name: pair_mask[i,k] = valid[i] * valid[k] for a 0/1 vector valid over the 1024 tokens of the crop; exactly 256 tokens are invalid.
All inputs are finite; a program needn't handle non-finite values.
Results may differ from the reference program's by a relative error of at most 0.0083.
Values may be sent and summed in bfloat16 or wider, within the bound.
A program may use at most 128 MiB of HBM per device.

```python
import jax
import jax.numpy as jnp
from jax import lax

CZ = 128
CH = 128
N = 1024
N_ROW = 8


def draw_pair_mask(key, part):
    key = jax.random.fold_in(key, 11)
    order = jax.random.permutation(key, N)
    valid = (order >= N // 4).astype(jnp.int32)
    return valid[:, None] * valid[None, :]


def block_levels(own_key, shape, shards, low, largest):
    def one(axis_at, parts):
        heights = jax.random.uniform(jax.random.fold_in(jax.random.fold_in(own_key, 6), axis_at), (parts,), jnp.float32, low / len(shards), largest / len(shards))
        return jnp.repeat(jnp.exp(heights), shape[axis_at] // parts).reshape((-1,) + (1,) * (len(shape) - axis_at - 1))

    loudness = one(*shards[0])
    for cut in shards[1:]:
        loudness = loudness * one(*cut)
    return loudness


def bell_draw(own_key, dims, scale, limit, cuts=(), dtype=jnp.bfloat16):
    array = jax.random.normal(own_key, dims, jnp.float32) * scale
    if len(cuts) > 0:
        array = block_levels(own_key, dims, cuts, -0.22, 0.18) * array
    return jnp.clip(array, min=-limit, max=limit).astype(dtype)


def setup_inputs(seed: int = 0, part: int = 0) -> dict:
    splits = jax.random.split(jax.random.key(seed), 9)
    part_splits = jax.random.split(jax.random.fold_in(splits[8], part), 9)
    pair_rep = bell_draw(part_splits[0], (N, N, CZ), 1.0, 6.0, ((0, 8), (1, 8)))
    pair_mask = draw_pair_mask(jax.random.fold_in(jax.random.fold_in(splits[8], part), 71), part)
    w_left_gate = bell_draw(splits[2], (CZ, CH), CZ ** -0.5, 0.5)
    w_left_proj = bell_draw(splits[3], (CZ, CH), CZ ** -0.5, 0.5)
    w_right_gate = bell_draw(splits[4], (CZ, CH), CZ ** -0.5, 0.5)
    w_right_proj = bell_draw(splits[5], (CZ, CH), CZ ** -0.5, 0.5)
    w_gate = bell_draw(splits[6], (CZ, CZ), CZ ** -0.5, 0.5)
    w_out = bell_draw(splits[7], (CH, CZ), CH ** -0.5, 0.5)
    return {"pair_rep": pair_rep, "pair_mask": pair_mask, "w_left_gate": w_left_gate, "w_left_proj": w_left_proj, "w_right_gate": w_right_gate, "w_right_proj": w_right_proj, "w_gate": w_gate, "w_out": w_out}


def normalize(values, along):
    average = lax.optimization_barrier(jnp.mean(values, along, keepdims=True))
    centre = values - average
    spread = lax.optimization_barrier(jnp.mean(centre * centre, along, keepdims=True))
    return centre * lax.rsqrt(spread + 1e-05)

def reference(pair_rep, pair_mask, w_left_gate, w_left_proj, w_right_gate, w_right_proj, w_gate, w_out):
    extent = pair_rep.shape[0]
    stripe = extent // N_ROW
    blocks = pair_rep.reshape(N_ROW, stripe, extent, CZ)
    mask_rows = pair_mask.reshape(N_ROW, stripe, extent)

    def both_sides(member):
        slab, masking = member
        normed = normalize(slab.astype(jnp.float32), 2).astype(jnp.bfloat16).reshape(stripe * extent, CZ)
        weight = masking.astype(jnp.float32).reshape(stripe * extent, 1)

        def project(gate_matrix, proj_matrix):
            gate_term = jnp.dot(normed, gate_matrix, preferred_element_type=jnp.float32)
            proj_term = jnp.dot(normed, proj_matrix, preferred_element_type=jnp.float32)
            return (jax.nn.sigmoid(gate_term) * proj_term * weight).astype(jnp.bfloat16).reshape(stripe, extent, CH)
        return (project(w_left_gate, w_left_proj), project(w_right_gate, w_right_proj))
    left_side, right_side = lax.map(both_sides, (blocks, mask_rows))
    left_side = left_side.reshape(extent, extent, CH).transpose(2, 0, 1)
    right_side = right_side.reshape(extent, extent, CH).transpose(2, 0, 1)

    def contract(member):
        left_one, right_one = member
        return jnp.dot(left_one, right_one.T, preferred_element_type=jnp.float32).astype(jnp.bfloat16)
    product = lax.map(contract, (left_side, right_side))
    by_rows = product.reshape(CH, N_ROW, stripe, extent).transpose(1, 0, 2, 3)

    def finish_rows(member):
        slab, mixed_slab = member
        normed = normalize(slab.astype(jnp.float32), 2).astype(jnp.bfloat16).reshape(stripe * extent, CZ)
        gate_values = jax.nn.sigmoid(jnp.dot(normed, w_gate, preferred_element_type=jnp.float32))
        mixed_norm = normalize(mixed_slab.astype(jnp.float32), 0).astype(jnp.bfloat16).reshape(CH, stripe * extent)
        result = gate_values * jnp.dot(mixed_norm.T, w_out, preferred_element_type=jnp.float32)
        return result.astype(jnp.bfloat16).reshape(stripe, extent, CZ)
    return lax.map(finish_rows, (blocks, by_rows)).reshape(extent, extent, CZ)
```

```python
import functools

import jax
import jax.numpy as jnp
from jax import lax
from jax.experimental import pallas as pl
from jax.experimental.pallas import tpu as pltpu
from jax.sharding import PartitionSpec as P

MESH = pl.DeviceIdType.MESH
EPS = 1e-05
VALID = 768
BF = jnp.bfloat16
F32 = jnp.float32


def dot(a, b):
    return jnp.dot(a, b, preferred_element_type=F32)


def dot_t(a, b):
    return lax.dot_general(a, b, (((1,), (1,)), ((), ())), preferred_element_type=F32)


def sigmoid(v):
    return 0.5 * jnp.tanh(0.5 * v) + 0.5


def normalize(v):
    centre = v - jnp.mean(v, axis=0, keepdims=True)
    spread = jnp.mean(centre * centre, axis=0, keepdims=True)
    return centre * lax.rsqrt(spread + EPS)


def wait(ref, sem):
    pltpu.make_async_copy(ref, ref, sem).wait()


def kernel(
    nr, nc, nq,
    x_hbm, mask_ref, wlg_ref, wlp_ref, wrg_ref, wrp_ref, wg_ref, wo_ref,
    out_hbm,
    field, normed, send_r, send_l, recv_r, recv_l, put_r, put_l, got_r, got_l,
    packed_r, prod, back, pick, w_t, maskf, vmine, vrow, vall, perm, eye,
    sem_x, sem_out, sem_v, a_send, a_recv, b_send, br_recv, bl_recv, p_send, p_recv, e_send, e_recv,
):
    row = lax.axis_index("row")
    col = lax.axis_index("col")
    ti, tk = mask_ref.shape
    ch = w_t.shape[1]
    cc = ch // nc
    dc = cc // nr
    qi = ti // nq
    full = nc * tk
    group = 4

    def col_peer(d):
        return lax.rem(col + d, nc)

    def row_peer(d):
        return lax.rem(row + d, nr)

    def x_copy(q):
        part = pl.ds(pl.multiple_of(q * qi, qi), qi)
        return pltpu.make_async_copy(x_hbm.at[part], field.at[part], sem_x.at[q])

    def out_copy(q):
        part = pl.ds(pl.multiple_of(q * qi, qi), qi)
        return pltpu.make_async_copy(send_r.at[part], out_hbm.at[part], sem_out.at[q])

    for q in range(nq):
        x_copy(q).start()

    barrier = pltpu.get_barrier_semaphore()
    for d in range(1, nc):
        pl.semaphore_signal(barrier, inc=1, device_id={"col": col_peer(d)}, device_id_type=MESH)
    for d in range(1, nr):
        pl.semaphore_signal(barrier, inc=1, device_id={"row": row_peer(d)}, device_id_type=MESH)

    eye[...] = (
        lax.broadcasted_iota(jnp.int32, (ch, ch), 0) == lax.broadcasted_iota(jnp.int32, (ch, ch), 1)
    ).astype(F32).astype(BF)
    at = lax.broadcasted_iota(jnp.int32, (cc * 16, cc * 16), 0)
    of = lax.broadcasted_iota(jnp.int32, (cc * 16, cc * 16), 1)
    perm[...] = (of == (at % 16) * cc + at // 16).astype(F32).astype(BF)
    for n, ref in enumerate((wrg_ref, wrp_ref, wlg_ref, wlp_ref, wg_ref, wo_ref)):
        w_t[n] = dot_t(eye[...], ref[...]).astype(BF)
    maskf[...] = mask_ref[...].astype(F32)
    vmine[...] = jnp.broadcast_to(jnp.max(maskf[...], axis=0, keepdims=True), vmine.shape)

    pl.semaphore_wait(barrier, nc - 1 + nr - 1)

    mine = pl.ds(pl.multiple_of(col * tk, tk), tk)
    for d in range(1, nc):
        pltpu.make_async_remote_copy(
            vmine, vrow.at[:, mine], sem_v.at[0], sem_v.at[1],
            device_id={"col": col_peer(d)}, device_id_type=MESH,
        ).start()
    pltpu.make_async_copy(vmine, vrow.at[:, mine], sem_v.at[1]).start()

    def lanes(ref, i):
        return jnp.concatenate([ref[i + g] for g in range(group)], axis=1)

    def edges(n, vals, i, dst):
        g = dot(w_t[n], vals)
        p = dot(w_t[n + 1], vals)
        m = jnp.concatenate([maskf[pl.ds(i + h, 1), :] for h in range(group)], axis=1)
        e = (sigmoid(g) * p * m).astype(BF)
        for h in range(group):
            dst[i + h] = e[:, h * tk:(h + 1) * tk]

    def compute_r(q):
        def body(t, carry):
            i = q * qi + t * group
            x = field[pl.ds(i, group)].reshape(group * tk, ch)
            vals = normalize(dot_t(eye[...], x)).astype(BF)
            for h in range(group):
                normed[i + h] = vals[:, h * tk:(h + 1) * tk]
            edges(0, vals, i, send_r)
            return carry

        lax.fori_loop(0, qi // group, body, 0)

    def compute_l(q):
        def body(t, carry):
            i = q * qi + t * group
            edges(2, lanes(normed, i), i, send_l)
            return carry

        lax.fori_loop(0, qi // group, body, 0)

    def start_a(n, q, src, dst):
        part = pl.ds(pl.multiple_of(q * qi, qi), qi)
        for d in range(1, nc):
            to = col_peer(d)
            pltpu.make_async_remote_copy(
                src.at[part, pl.ds(pl.multiple_of(to * cc, cc), cc), :], dst.at[part, :, mine],
                a_send.at[n, q], a_recv.at[n, q],
                device_id={"col": to}, device_id_type=MESH,
            ).start()
        pltpu.make_async_copy(
            src.at[part, pl.ds(pl.multiple_of(col * cc, cc), cc), :], dst.at[part, :, mine],
            a_recv.at[n, q],
        ).start()

    def compact(n, q, src, dst):
        part = pl.ds(pl.multiple_of(q * qi, qi), qi)
        wait(src.at[part], a_recv.at[n, q])

        def body(t, carry):
            i = pl.multiple_of(q * qi + t * 16, 16)
            a = src[pl.ds(i, 16)].reshape(16 * cc, full)
            b = dot(perm[...], dot_t(a, pick[...]).astype(BF)).astype(BF)
            dst[:, pl.ds(i, 16), :] = b.reshape(cc, 16, VALID)
            return carry

        lax.fori_loop(0, qi // 16, body, 0)

    def start_b(n, q, src, dst_at, recv):
        part = pl.ds(pl.multiple_of(q * qi, qi), qi)
        for d in range(1, nr):
            to = row_peer(d)
            pltpu.make_async_remote_copy(
                src.at[pl.ds(to * dc, dc), part, :], dst_at, b_send.at[n, q], recv,
                device_id={"row": to}, device_id_type=MESH,
            ).start()
        pltpu.make_async_copy(src.at[pl.ds(row * dc, dc), part, :], dst_at, recv).start()

    def ranks(v):
        a = lax.broadcasted_iota(jnp.int32, (tk, tk), 0)
        b = lax.broadcasted_iota(jnp.int32, (tk, tk), 1)
        upto = (a <= b).astype(F32).astype(BF)
        ones = jnp.ones((tk, tk), BF)
        base = jnp.zeros((v.shape[0], tk), F32)
        out = []
        for n in range(nc):
            block = v[:, n * tk:(n + 1) * tk]
            block16 = block.astype(BF)
            rank = dot(block16, upto) + base - 1.0
            out.append(jnp.where(block > 0.5, rank, -1.0))
            base = base + dot(block16, ones)
        return jnp.concatenate(out, axis=1)

    def fill_pick(v):
        rank = ranks(v)[0:1, :].astype(jnp.int32)

        def body(t, carry):
            p = pl.multiple_of(t * 16, 16)
            place = lax.broadcasted_iota(jnp.int32, (16, full), 0) + p
            pick[pl.ds(p, 16), :] = (place == rank).astype(F32).astype(BF)
            return carry

        lax.fori_loop(0, VALID // 16, body, 0)

    def step_r(q, carry):
        x_copy(q).wait()
        compute_r(q)
        start_a(0, q, send_r, recv_r)
        return carry

    lax.fori_loop(0, nq, step_r, 0)

    wait(vrow, sem_v.at[1])
    fill_pick(vrow[...])
    for d in range(1, nr):
        pltpu.make_async_remote_copy(
            vrow, vall.at[row], sem_v.at[2], sem_v.at[3],
            device_id={"row": row_peer(d)}, device_id_type=MESH,
        ).start()
    pltpu.make_async_copy(vrow, vall.at[row], sem_v.at[3]).start()

    def step_l(q, carry):
        compute_l(q)
        compact(0, q, recv_r, put_r)
        mine_rows = pl.ds(pl.multiple_of(row * ti + q * qi, qi), qi)
        start_b(0, q, put_r, got_r.at[:, mine_rows, :], br_recv)
        start_a(1, q, send_l, recv_l)
        return carry

    lax.fori_loop(0, nq, step_l, 0)

    def step_c(q, carry):
        compact(1, q, recv_l, put_l)
        start_b(1, q, put_l, got_l.at[q, :, pl.ds(pl.multiple_of(row * qi, qi), qi), :], bl_recv.at[q])
        return carry

    lax.fori_loop(0, nq, step_c, 0)

    wait(vall, sem_v.at[3])
    fill_pick(jnp.max(vall[...], axis=0))
    wait(got_r, br_recv)

    def pack(t, carry):
        p = pl.multiple_of(t * 256, 256)
        for n in range(dc):
            packed_r[n, pl.ds(p, 256), :] = dot(pick[pl.ds(p, 256), :], got_r[n]).astype(BF)
        return carry

    lax.fori_loop(0, VALID // 256, pack, 0)

    def step_p(q, carry):
        wait(got_l.at[q], bl_recv.at[q])
        for n in range(dc):
            prod[q, n] = dot_t(got_l[q, n], packed_r[n]).astype(BF)
        dst = back.at[q, pl.ds(row * dc, dc)]
        for d in range(1, nr):
            to = row_peer(d)
            pltpu.make_async_remote_copy(
                prod.at[q, :, pl.ds(pl.multiple_of(to * qi, qi), qi), :], dst,
                p_send.at[q], p_recv.at[q],
                device_id={"row": to}, device_id_type=MESH,
            ).start()
        pltpu.make_async_copy(
            prod.at[q, :, pl.ds(pl.multiple_of(row * qi, qi), qi), :], dst, p_recv.at[q]
        ).start()
        return carry

    lax.fori_loop(0, nq, step_p, 0)

    def step_e(q, carry):
        part = pl.ds(pl.multiple_of(q * qi, qi), qi)
        wait(send_l.at[pl.ds(0, qi * (nc - 1) // nc)], a_send.at[1, q])
        wait(send_r.at[pl.ds(0, qi * (nc - 1) // nc)], a_send.at[0, q])
        wait(back.at[q], p_recv.at[q])

        def body(t, carry):
            i = pl.multiple_of(q * qi + t * 16, 16)
            a = back[q, :, pl.ds(pl.multiple_of(t * 16, 16), 16), :].reshape(16 * cc, VALID)
            e = dot(dot(perm[...], a).astype(BF), pick[...]).astype(BF)
            for n in range(nc):
                send_l[pl.ds(i, 16), n * cc:(n + 1) * cc, :] = e[:, n * tk:(n + 1) * tk].reshape(16, cc, tk)
            return carry

        lax.fori_loop(0, qi // 16, body, 0)
        dst = field.at[part, pl.ds(pl.multiple_of(col * cc, cc), cc), :]
        for d in range(1, nc):
            to = col_peer(d)
            pltpu.make_async_remote_copy(
                send_l.at[part, pl.ds(pl.multiple_of(to * cc, cc), cc), :], dst,
                e_send.at[q], e_recv.at[q],
                device_id={"col": to}, device_id_type=MESH,
            ).start()
        pltpu.make_async_copy(
            send_l.at[part, pl.ds(pl.multiple_of(col * cc, cc), cc), :], dst, e_recv.at[q]
        ).start()
        return carry

    lax.fori_loop(0, nq, step_e, 0)

    def step_f(q, carry):
        part = pl.ds(pl.multiple_of(q * qi, qi), qi)
        wait(field.at[part], e_recv.at[q])

        def body(t, carry):
            i = q * qi + t * group
            mixed = normalize(lanes(field, i).astype(F32)).astype(BF)
            u = (sigmoid(dot(w_t[4], lanes(normed, i))) * dot(w_t[5], mixed)).astype(BF)
            for h in range(group):
                send_r[i + h] = dot_t(eye[...], u[:, h * tk:(h + 1) * tk]).astype(BF)
            return carry

        lax.fori_loop(0, qi // group, body, 0)
        out_copy(q).start()
        return carry

    lax.fori_loop(0, nq, step_f, 0)

    wait(vrow.at[:, pl.ds(0, full - tk)], sem_v.at[0])
    wait(vall.at[pl.ds(0, nr - 1)], sem_v.at[2])

    def finish(q, carry):
        wait(put_r.at[pl.ds(0, dc * (nr - 1)), pl.ds(0, qi), :], b_send.at[0, q])
        wait(put_l.at[pl.ds(0, dc * (nr - 1)), pl.ds(0, qi), :], b_send.at[1, q])
        wait(prod.at[0, :, pl.ds(0, qi * (nr - 1)), :], p_send.at[q])
        wait(send_l.at[pl.ds(0, qi * (nc - 1) // nc)], e_send.at[q])
        out_copy(q).wait()
        return carry

    lax.fori_loop(0, nq, finish, 0)


def solution(mesh):
    nr, nc = mesh.shape["row"], mesh.shape["col"]
    nq = 4

    def on_device(pair_rep, pair_mask, w_left_gate, w_left_proj, w_right_gate, w_right_proj, w_gate, w_out):
        ti, tk, cz = pair_rep.shape
        ch = w_left_gate.shape[1]
        cc, dc = ch // nc, ch // nc // nr
        qi = ti // nq
        tile = pltpu.VMEM((ti, ch, tk), BF)
        sem = pltpu.SemaphoreType.DMA
        vmem = pl.BlockSpec(memory_space=pltpu.VMEM)
        return pl.pallas_call(
            functools.partial(kernel, nr, nc, nq),
            out_shape=jax.ShapeDtypeStruct(pair_rep.shape, pair_rep.dtype),
            in_specs=[pl.BlockSpec(memory_space=pl.ANY)] + [vmem] * 7,
            out_specs=pl.BlockSpec(memory_space=pl.ANY),
            scratch_shapes=[
                tile, tile, tile, tile,
                pltpu.VMEM((ti, cc, nc * tk), BF), pltpu.VMEM((ti, cc, nc * tk), BF),
                pltpu.VMEM((cc, ti, VALID), BF), pltpu.VMEM((cc, ti, VALID), BF),
                pltpu.VMEM((dc, nr * ti, VALID), BF), pltpu.VMEM((nq, dc, nr * qi, VALID), BF),
                pltpu.VMEM((dc, VALID, VALID), BF),
                pltpu.VMEM((nq, dc, nr * qi, VALID), BF),
                pltpu.VMEM((nq, cc, qi, VALID), BF),
                pltpu.VMEM((VALID, nc * tk), BF),
                pltpu.VMEM((6, ch, cz), BF),
                pltpu.VMEM((ti, tk), F32), pltpu.VMEM((8, tk), F32),
                pltpu.VMEM((8, nc * tk), F32), pltpu.VMEM((nr, 8, nc * tk), F32),
                pltpu.VMEM((16 * cc, 16 * cc), BF), pltpu.VMEM((ch, ch), BF),
                sem((nq,)), sem((nq,)), sem((4,)), sem((2, nq)), sem((2, nq)), sem((2, nq)),
                sem(()), sem((nq,)), sem((nq,)), sem((nq,)), sem((nq,)), sem((nq,)),
            ],
            compiler_params=pltpu.CompilerParams(
                collective_id=0, has_side_effects=True, vmem_limit_bytes=58 << 20
            ),
        )(pair_rep, pair_mask, w_left_gate, w_left_proj, w_right_gate, w_right_proj, w_gate, w_out)

    in_specs = (P(("dp", "row"), "col", None), P(("dp", "row"), "col")) + (P(),) * 6
    return jax.shard_map(
        on_device, mesh=mesh, in_specs=in_specs, out_specs=P(("dp", "row"), "col", None), check_vma=False
    )
```

```python
import functools

import jax
import jax.numpy as jnp
from jax import lax
from jax.experimental import pallas as pl
from jax.experimental.pallas import tpu as pltpu
from jax.sharding import PartitionSpec as P

MESH = pl.DeviceIdType.MESH
EPS = 1e-05
VALID = 768
BF = jnp.bfloat16
F32 = jnp.float32


def dot(a, b):
    return jnp.dot(a, b, preferred_element_type=F32)


def dot_t(a, b):
    return lax.dot_general(a, b, (((1,), (1,)), ((), ())), preferred_element_type=F32)


def sigmoid(v):
    return 0.5 * jnp.tanh(0.5 * v) + 0.5


def normalize(v):
    centre = v - jnp.mean(v, axis=0, keepdims=True)
    spread = jnp.mean(centre * centre, axis=0, keepdims=True)
    return centre * lax.rsqrt(spread + EPS)


def wait(ref, sem):
    pltpu.make_async_copy(ref, ref, sem).wait()


def kernel(
    nr, nc, nq,
    x_hbm, mask_ref, wlg_ref, wlp_ref, wrg_ref, wrp_ref, wg_ref, wo_ref,
    out_hbm,
    field, normed, send_r, send_l, recv_r, recv_l, put_r, put_l, got_r, got_l,
    packed_r, prod, back, pick, w_t, maskf, vmine, vrow, vall, perm, eye,
    sem_x, sem_out, sem_v, a_send, a_recv, b_send, br_recv, bl_recv, p_send, p_recv, e_send, e_recv,
):
    row = lax.axis_index("row")
    col = lax.axis_index("col")
    ti, tk = mask_ref.shape
    ch = w_t.shape[1]
    cc = ch // nc
    dc = cc // nr
    qi = ti // nq
    full = nc * tk
    group = 8

    def col_peer(d):
        return lax.rem(col + d, nc)

    def row_peer(d):
        return lax.rem(row + d, nr)

    def x_copy(q):
        part = pl.ds(pl.multiple_of(q * qi, qi), qi)
        return pltpu.make_async_copy(x_hbm.at[part], field.at[part], sem_x.at[q])

    def out_copy(q):
        part = pl.ds(pl.multiple_of(q * qi, qi), qi)
        return pltpu.make_async_copy(send_r.at[part], out_hbm.at[part], sem_out.at[q])

    for q in range(nq):
        x_copy(q).start()

    barrier = pltpu.get_barrier_semaphore()
    for d in range(1, nc):
        pl.semaphore_signal(barrier, inc=1, device_id={"col": col_peer(d)}, device_id_type=MESH)
    for d in range(1, nr):
        pl.semaphore_signal(barrier, inc=1, device_id={"row": row_peer(d)}, device_id_type=MESH)

    eye[...] = (
        lax.broadcasted_iota(jnp.int32, (ch, ch), 0) == lax.broadcasted_iota(jnp.int32, (ch, ch), 1)
    ).astype(F32).astype(BF)
    at = lax.broadcasted_iota(jnp.int32, (cc * 16, cc * 16), 0)
    of = lax.broadcasted_iota(jnp.int32, (cc * 16, cc * 16), 1)
    perm[...] = (of == (at % 16) * cc + at // 16).astype(F32).astype(BF)
    for n, ref in enumerate((wrg_ref, wrp_ref, wlg_ref, wlp_ref, wg_ref, wo_ref)):
        w_t[n] = dot_t(eye[...], ref[...]).astype(BF)
    maskf[...] = mask_ref[...].astype(F32)
    vmine[...] = jnp.broadcast_to(jnp.max(maskf[...], axis=0, keepdims=True), vmine.shape)

    pl.semaphore_wait(barrier, nc - 1 + nr - 1)

    mine = pl.ds(pl.multiple_of(col * tk, tk), tk)
    for d in range(1, nc):
        pltpu.make_async_remote_copy(
            vmine, vrow.at[:, mine], sem_v.at[0], sem_v.at[1],
            device_id={"col": col_peer(d)}, device_id_type=MESH,
        ).start()
    pltpu.make_async_copy(vmine, vrow.at[:, mine], sem_v.at[1]).start()

    def lanes(ref, i):
        return jnp.concatenate([ref[i + g] for g in range(group)], axis=1)

    def edges(n, vals, i, dst):
        g = dot(w_t[n], vals)
        p = dot(w_t[n + 1], vals)
        m = jnp.concatenate([maskf[pl.ds(i + h, 1), :] for h in range(group)], axis=1)
        e = (sigmoid(g) * p * m).astype(BF)
        for h in range(group):
            dst[i + h] = e[:, h * tk:(h + 1) * tk]

    def compute_r(q):
        def body(t, carry):
            i = q * qi + t * group
            x = field[pl.ds(i, group)].reshape(group * tk, ch)
            vals = normalize(dot_t(eye[...], x)).astype(BF)
            for h in range(group):
                normed[i + h] = vals[:, h * tk:(h + 1) * tk]
            edges(0, vals, i, send_r)
            return carry

        lax.fori_loop(0, qi // group, body, 0)

    def compute_l(q):
        def body(t, carry):
            i = q * qi + t * group
            edges(2, lanes(normed, i), i, send_l)
            return carry

        lax.fori_loop(0, qi // group, body, 0)

    def start_a(n, q, src, dst):
        part = pl.ds(pl.multiple_of(q * qi, qi), qi)
        for d in range(1, nc):
            to = col_peer(d)
            pltpu.make_async_remote_copy(
                src.at[part, pl.ds(pl.multiple_of(to * cc, cc), cc), :], dst.at[part, :, mine],
                a_send.at[n, q], a_recv.at[n, q],
                device_id={"col": to}, device_id_type=MESH,
            ).start()
        pltpu.make_async_copy(
            src.at[part, pl.ds(pl.multiple_of(col * cc, cc), cc), :], dst.at[part, :, mine],
            a_recv.at[n, q],
        ).start()

    def compact(n, q, src, dst):
        part = pl.ds(pl.multiple_of(q * qi, qi), qi)
        wait(src.at[part], a_recv.at[n, q])

        def body(t, carry):
            i = pl.multiple_of(q * qi + t * 16, 16)
            a = src[pl.ds(i, 16)].reshape(16 * cc, full)
            b = dot(perm[...], dot_t(a, pick[...]).astype(BF)).astype(BF)
            dst[:, pl.ds(i, 16), :] = b.reshape(cc, 16, VALID)
            return carry

        lax.fori_loop(0, qi // 16, body, 0)

    def start_b(n, q, src, dst_at, recv):
        part = pl.ds(pl.multiple_of(q * qi, qi), qi)
        for d in range(1, nr):
            to = row_peer(d)
            pltpu.make_async_remote_copy(
                src.at[pl.ds(to * dc, dc), part, :], dst_at, b_send.at[n, q], recv,
                device_id={"row": to}, device_id_type=MESH,
            ).start()
        pltpu.make_async_copy(src.at[pl.ds(row * dc, dc), part, :], dst_at, recv).start()

    def ranks(v):
        a = lax.broadcasted_iota(jnp.int32, (tk, tk), 0)
        b = lax.broadcasted_iota(jnp.int32, (tk, tk), 1)
        upto = (a <= b).astype(F32).astype(BF)
        ones = jnp.ones((tk, tk), BF)
        base = jnp.zeros((v.shape[0], tk), F32)
        out = []
        for n in range(nc):
            block = v[:, n * tk:(n + 1) * tk]
            block16 = block.astype(BF)
            rank = dot(block16, upto) + base - 1.0
            out.append(jnp.where(block > 0.5, rank, -1.0))
            base = base + dot(block16, ones)
        return jnp.concatenate(out, axis=1)

    def fill_pick(v):
        rank = ranks(v)[0:1, :].astype(jnp.int32)

        def body(t, carry):
            p = pl.multiple_of(t * 16, 16)
            place = lax.broadcasted_iota(jnp.int32, (16, full), 0) + p
            pick[pl.ds(p, 16), :] = (place == rank).astype(F32).astype(BF)
            return carry

        lax.fori_loop(0, VALID // 16, body, 0)

    def step_r(q, carry):
        x_copy(q).wait()
        compute_r(q)
        start_a(0, q, send_r, recv_r)
        return carry

    lax.fori_loop(0, nq, step_r, 0)

    wait(vrow, sem_v.at[1])
    fill_pick(vrow[...])
    for d in range(1, nr):
        pltpu.make_async_remote_copy(
            vrow, vall.at[row], sem_v.at[2], sem_v.at[3],
            device_id={"row": row_peer(d)}, device_id_type=MESH,
        ).start()
    pltpu.make_async_copy(vrow, vall.at[row], sem_v.at[3]).start()

    def step_l(q, carry):
        compact(0, q, recv_r, put_r)
        mine_rows = pl.ds(pl.multiple_of(row * ti + q * qi, qi), qi)
        start_b(0, q, put_r, got_r.at[:, mine_rows, :], br_recv)
        compute_l(q)
        start_a(1, q, send_l, recv_l)
        return carry

    lax.fori_loop(0, nq, step_l, 0)

    def step_c(q, carry):
        compact(1, q, recv_l, put_l)
        start_b(1, q, put_l, got_l.at[q, :, pl.ds(pl.multiple_of(row * qi, qi), qi), :], bl_recv.at[q])
        return carry

    lax.fori_loop(0, nq, step_c, 0)

    wait(vall, sem_v.at[3])
    fill_pick(jnp.max(vall[...], axis=0))
    wait(got_r, br_recv)

    def pack(t, carry):
        p = pl.multiple_of(t * 256, 256)
        for n in range(dc):
            packed_r[n, pl.ds(p, 256), :] = dot(pick[pl.ds(p, 256), :], got_r[n]).astype(BF)
        return carry

    lax.fori_loop(0, VALID // 256, pack, 0)

    def step_p(q, carry):
        wait(got_l.at[q], bl_recv.at[q])
        for n in range(dc):
            prod[q, n] = dot_t(got_l[q, n], packed_r[n]).astype(BF)
        dst = back.at[q, pl.ds(row * dc, dc)]
        for d in range(1, nr):
            to = row_peer(d)
            pltpu.make_async_remote_copy(
                prod.at[q, :, pl.ds(pl.multiple_of(to * qi, qi), qi), :], dst,
                p_send.at[q], p_recv.at[q],
                device_id={"row": to}, device_id_type=MESH,
            ).start()
        pltpu.make_async_copy(
            prod.at[q, :, pl.ds(pl.multiple_of(row * qi, qi), qi), :], dst, p_recv.at[q]
        ).start()
        return carry

    lax.fori_loop(0, nq, step_p, 0)

    def step_e(q, carry):
        part = pl.ds(pl.multiple_of(q * qi, qi), qi)
        wait(send_l.at[pl.ds(0, qi * (nc - 1) // nc)], a_send.at[1, q])
        wait(send_r.at[pl.ds(0, qi * (nc - 1) // nc)], a_send.at[0, q])
        wait(back.at[q], p_recv.at[q])

        def body(t, carry):
            i = pl.multiple_of(q * qi + t * 16, 16)
            a = back[q, :, pl.ds(pl.multiple_of(t * 16, 16), 16), :].reshape(16 * cc, VALID)
            e = dot(dot(perm[...], a).astype(BF), pick[...]).astype(BF)
            for n in range(nc):
                send_l[pl.ds(i, 16), n * cc:(n + 1) * cc, :] = e[:, n * tk:(n + 1) * tk].reshape(16, cc, tk)
            return carry

        lax.fori_loop(0, qi // 16, body, 0)
        dst = field.at[part, pl.ds(pl.multiple_of(col * cc, cc), cc), :]
        for d in range(1, nc):
            to = col_peer(d)
            pltpu.make_async_remote_copy(
                send_l.at[part, pl.ds(pl.multiple_of(to * cc, cc), cc), :], dst,
                e_send.at[q], e_recv.at[q],
                device_id={"col": to}, device_id_type=MESH,
            ).start()
        pltpu.make_async_copy(
            send_l.at[part, pl.ds(pl.multiple_of(col * cc, cc), cc), :], dst, e_recv.at[q]
        ).start()
        return carry

    lax.fori_loop(0, nq, step_e, 0)

    def step_f(q, carry):
        part = pl.ds(pl.multiple_of(q * qi, qi), qi)
        wait(field.at[part], e_recv.at[q])

        def body(t, carry):
            i = q * qi + t * group
            mixed = normalize(lanes(field, i).astype(F32)).astype(BF)
            u = (sigmoid(dot(w_t[4], lanes(normed, i))) * dot(w_t[5], mixed)).astype(BF)
            for h in range(group):
                send_r[i + h] = dot_t(eye[...], u[:, h * tk:(h + 1) * tk]).astype(BF)
            return carry

        lax.fori_loop(0, qi // group, body, 0)
        out_copy(q).start()
        return carry

    lax.fori_loop(0, nq, step_f, 0)

    wait(vrow.at[:, pl.ds(0, full - tk)], sem_v.at[0])
    wait(vall.at[pl.ds(0, nr - 1)], sem_v.at[2])

    def finish(q, carry):
        wait(put_r.at[pl.ds(0, dc * (nr - 1)), pl.ds(0, qi), :], b_send.at[0, q])
        wait(put_l.at[pl.ds(0, dc * (nr - 1)), pl.ds(0, qi), :], b_send.at[1, q])
        wait(prod.at[0, :, pl.ds(0, qi * (nr - 1)), :], p_send.at[q])
        wait(send_l.at[pl.ds(0, qi * (nc - 1) // nc)], e_send.at[q])
        out_copy(q).wait()
        return carry

    lax.fori_loop(0, nq, finish, 0)


def solution(mesh):
    nr, nc = mesh.shape["row"], mesh.shape["col"]
    nq = 8

    def on_device(pair_rep, pair_mask, w_left_gate, w_left_proj, w_right_gate, w_right_proj, w_gate, w_out):
        ti, tk, cz = pair_rep.shape
        ch = w_left_gate.shape[1]
        cc, dc = ch // nc, ch // nc // nr
        qi = ti // nq
        tile = pltpu.VMEM((ti, ch, tk), BF)
        sem = pltpu.SemaphoreType.DMA
        vmem = pl.BlockSpec(memory_space=pltpu.VMEM)
        return pl.pallas_call(
            functools.partial(kernel, nr, nc, nq),
            out_shape=jax.ShapeDtypeStruct(pair_rep.shape, pair_rep.dtype),
            in_specs=[pl.BlockSpec(memory_space=pl.ANY)] + [vmem] * 7,
            out_specs=pl.BlockSpec(memory_space=pl.ANY),
            scratch_shapes=[
                tile, tile, tile, tile,
                pltpu.VMEM((ti, cc, nc * tk), BF), pltpu.VMEM((ti, cc, nc * tk), BF),
                pltpu.VMEM((cc, ti, VALID), BF), pltpu.VMEM((cc, ti, VALID), BF),
                pltpu.VMEM((dc, nr * ti, VALID), BF), pltpu.VMEM((nq, dc, nr * qi, VALID), BF),
                pltpu.VMEM((dc, VALID, VALID), BF),
                pltpu.VMEM((nq, dc, nr * qi, VALID), BF),
                pltpu.VMEM((nq, cc, qi, VALID), BF),
                pltpu.VMEM((VALID, nc * tk), BF),
                pltpu.VMEM((6, ch, cz), BF),
                pltpu.VMEM((ti, tk), F32), pltpu.VMEM((8, tk), F32),
                pltpu.VMEM((8, nc * tk), F32), pltpu.VMEM((nr, 8, nc * tk), F32),
                pltpu.VMEM((16 * cc, 16 * cc), BF), pltpu.VMEM((ch, ch), BF),
                sem((nq,)), sem((nq,)), sem((4,)), sem((2, nq)), sem((2, nq)), sem((2, nq)),
                sem(()), sem((nq,)), sem((nq,)), sem((nq,)), sem((nq,)), sem((nq,)),
            ],
            compiler_params=pltpu.CompilerParams(
                collective_id=0, has_side_effects=True, vmem_limit_bytes=58 << 20
            ),
        )(pair_rep, pair_mask, w_left_gate, w_left_proj, w_right_gate, w_right_proj, w_gate, w_out)

    in_specs = (P(("dp", "row"), "col", None), P(("dp", "row"), "col")) + (P(),) * 6
    return jax.shard_map(
        on_device, mesh=mesh, in_specs=in_specs, out_specs=P(("dp", "row"), "col", None), check_vma=False
    )
```

```python
import functools

import jax
import jax.numpy as jnp
from jax import lax
from jax.experimental import pallas as pl
from jax.experimental.pallas import tpu as pltpu
from jax.sharding import PartitionSpec as P

MESH = pl.DeviceIdType.MESH
EPS = 1e-05
VALID = 768
BF = jnp.bfloat16
F32 = jnp.float32


def dot(a, b):
    return jnp.dot(a, b, preferred_element_type=F32)


def dot_t(a, b):
    return lax.dot_general(a, b, (((1,), (1,)), ((), ())), preferred_element_type=F32)


def sigmoid(v):
    return 0.5 * jnp.tanh(0.5 * v) + 0.5


def normalize(v):
    centre = v - jnp.mean(v, axis=0, keepdims=True)
    spread = jnp.mean(centre * centre, axis=0, keepdims=True)
    return centre * lax.rsqrt(spread + EPS)


def wait(ref, sem):
    pltpu.make_async_copy(ref, ref, sem).wait()


def kernel(
    nr, nc, nq,
    x_hbm, mask_ref, wlg_ref, wlp_ref, wrg_ref, wrp_ref, wg_ref, wo_ref,
    out_hbm,
    field, normed, send_r, send_l, recv_r, recv_l, put_r, put_l, got_r, got_l,
    packed_r, prod, back, pick, w_t, maskf, vmine, vrow, vall, perm, eye,
    sem_x, sem_out, sem_v, a_send, a_recv, b_send, br_recv, f_send, f_recv, bl_recv, p_send, p_recv, e_send, e_recv,
):
    row = lax.axis_index("row")
    col = lax.axis_index("col")
    ti, tk = mask_ref.shape
    ch = w_t.shape[1]
    cc = ch // nc
    dc = cc // nr
    qi = ti // nq
    full = nc * tk
    near = nr // 2
    ahead = nq // 2
    lag = 2
    group = 8

    def col_peer(d):
        return lax.rem(col + d, nc)

    def row_peer(d):
        return lax.rem(row + d + nr, nr)

    def x_copy(q):
        part = pl.ds(pl.multiple_of(q * qi, qi), qi)
        return pltpu.make_async_copy(x_hbm.at[part], field.at[part], sem_x.at[q])

    def out_copy(q):
        part = pl.ds(pl.multiple_of(q * qi, qi), qi)
        return pltpu.make_async_copy(send_r.at[part], out_hbm.at[part], sem_out.at[q])

    for q in range(nq):
        x_copy(q).start()

    barrier = pltpu.get_barrier_semaphore()
    for d in range(1, nc):
        pl.semaphore_signal(barrier, inc=1, device_id={"col": col_peer(d)}, device_id_type=MESH)
    for d in range(1, nr):
        pl.semaphore_signal(barrier, inc=1, device_id={"row": row_peer(d)}, device_id_type=MESH)

    eye[...] = (
        lax.broadcasted_iota(jnp.int32, (ch, ch), 0) == lax.broadcasted_iota(jnp.int32, (ch, ch), 1)
    ).astype(F32).astype(BF)
    at = lax.broadcasted_iota(jnp.int32, (cc * 16, cc * 16), 0)
    of = lax.broadcasted_iota(jnp.int32, (cc * 16, cc * 16), 1)
    perm[...] = (of == (at % 16) * cc + at // 16).astype(F32).astype(BF)
    for n, ref in enumerate((wrg_ref, wrp_ref, wlg_ref, wlp_ref, wg_ref, wo_ref)):
        w_t[n] = dot_t(eye[...], ref[...]).astype(BF)
    maskf[...] = mask_ref[...].astype(F32)
    vmine[...] = jnp.broadcast_to(jnp.max(maskf[...], axis=0, keepdims=True), vmine.shape)

    mine = pl.ds(pl.multiple_of(col * tk, tk), tk)

    def lanes(ref, i):
        return jnp.concatenate([ref[i + g] for g in range(group)], axis=1)

    def edges(n, vals, i, dst):
        g = dot(w_t[n], vals)
        p = dot(w_t[n + 1], vals)
        m = jnp.concatenate([maskf[pl.ds(i + h, 1), :] for h in range(group)], axis=1)
        e = (sigmoid(g) * p * m).astype(BF)
        for h in range(group):
            dst[i + h] = e[:, h * tk:(h + 1) * tk]

    def compute_r(q):
        def body(t, carry):
            i = q * qi + t * group
            x = field[pl.ds(i, group)].reshape(group * tk, ch)
            vals = normalize(dot_t(eye[...], x)).astype(BF)
            for h in range(group):
                normed[i + h] = vals[:, h * tk:(h + 1) * tk]
            edges(0, vals, i, send_r)
            return carry

        lax.fori_loop(0, qi // group, body, 0)

    def compute_l(q):
        def body(t, carry):
            i = q * qi + t * group
            edges(2, lanes(normed, i), i, send_l)
            return carry

        lax.fori_loop(0, qi // group, body, 0)

    def start_a(n, q, src, dst):
        part = pl.ds(pl.multiple_of(q * qi, qi), qi)
        for d in range(1, nc):
            to = col_peer(d)
            pltpu.make_async_remote_copy(
                src.at[part, pl.ds(pl.multiple_of(to * cc, cc), cc), :], dst.at[part, :, mine],
                a_send.at[n, q], a_recv.at[n, q],
                device_id={"col": to}, device_id_type=MESH,
            ).start()
        pltpu.make_async_copy(
            src.at[part, pl.ds(pl.multiple_of(col * cc, cc), cc), :], dst.at[part, :, mine],
            a_recv.at[n, q],
        ).start()

    def compact(n, q, src, dst):
        part = pl.ds(pl.multiple_of(q * qi, qi), qi)
        wait(src.at[part], a_recv.at[n, q])

        def body(t, carry):
            i = pl.multiple_of(q * qi + t * 16, 16)
            a = src[pl.ds(i, 16)].reshape(16 * cc, full)
            b = dot(perm[...], dot_t(a, pick[...]).astype(BF)).astype(BF)
            dst[:, pl.ds(i, 16), :] = b.reshape(cc, 16, VALID)
            return carry

        lax.fori_loop(0, qi // 16, body, 0)

    def start_near(piece, send, recv):
        for b in range(1, near):
            for slot_at, d in ((0, b), (1, -b)):
                src, dst = piece(slot_at, b)
                pltpu.make_async_remote_copy(
                    src, dst, send, recv, device_id={"row": row_peer(d)}, device_id_type=MESH
                ).start()

    def channels(g):
        return pl.ds(lax.rem(g + nr, nr) * dc, dc)

    def chunk(q):
        return pl.ds(pl.multiple_of(q * qi, qi), qi)

    def rows_of(r, q):
        return pl.ds(pl.multiple_of(lax.rem(r + nr, nr) * ti + q * qi, qi), qi)

    def send_right(q):
        def piece(slot, b):
            group_at = row + b if slot == 0 else row - b - 1
            return put_r.at[channels(group_at), chunk(q), :], got_r.at[slot, :, rows_of(row, q), :]

        start_near(piece, b_send.at[0, q], br_recv.at[q])
        for slot in range(2):
            src = put_r.at[channels(row - slot), chunk(q), :]
            pltpu.make_async_remote_copy(
                src, got_r.at[1 - slot, :, rows_of(row, q), :], b_send.at[0, q], f_recv,
                device_id={"row": row_peer(1 - 2 * slot)}, device_id_type=MESH,
            ).start()
            pltpu.make_async_copy(src, got_r.at[slot, :, rows_of(row, q), :], f_recv).start()

    def forward_right(q):
        wait(got_r.at[:, :, pl.ds(0, (near - 1) * qi), :], br_recv.at[q])
        for b in range(1, near):
            for slot in range(2):
                rows = rows_of(row - b if slot == 0 else row + b, q)
                pltpu.make_async_remote_copy(
                    got_r.at[slot, :, rows, :], got_r.at[1 - slot, :, rows, :], f_send.at[q], f_recv,
                    device_id={"row": row_peer(1 - 2 * slot)}, device_id_type=MESH,
                ).start()

    def send_left(q):
        def piece(slot, b):
            group_at = row + b if slot == 0 else row - b - 1
            return put_l.at[channels(group_at), chunk(q), :], got_l.at[q, slot, :, pl.ds(b * qi, qi), :]

        start_near(piece, b_send.at[1, q], bl_recv.at[q])
        for slot in range(2):
            pltpu.make_async_copy(
                put_l.at[channels(row - slot), chunk(q), :], got_l.at[q, slot, :, pl.ds(0, qi), :],
                bl_recv.at[q],
            ).start()

    def send_product(q):
        for b in range(near):
            for slot in range(2):
                src = prod.at[q, slot, :, pl.ds(b * qi, qi), :]
                dst = back.at[q, channels(row - slot)]
                if b == 0:
                    pltpu.make_async_copy(src, dst, p_recv.at[q]).start()
                else:
                    pltpu.make_async_remote_copy(
                        src, dst, p_send.at[q], p_recv.at[q],
                        device_id={"row": row_peer(-b if slot == 0 else b)}, device_id_type=MESH,
                    ).start()

    def ranks(v):
        a = lax.broadcasted_iota(jnp.int32, (tk, tk), 0)
        b = lax.broadcasted_iota(jnp.int32, (tk, tk), 1)
        upto = (a <= b).astype(F32).astype(BF)
        ones = jnp.ones((tk, tk), BF)
        base = jnp.zeros((v.shape[0], tk), F32)
        out = []
        for n in range(nc):
            block = v[:, n * tk:(n + 1) * tk]
            block16 = block.astype(BF)
            rank = dot(block16, upto) + base - 1.0
            out.append(jnp.where(block > 0.5, rank, -1.0))
            base = base + dot(block16, ones)
        return jnp.concatenate(out, axis=1)

    def fill_pick(v):
        rank = ranks(v)[0:1, :].astype(jnp.int32)

        def body(t, carry):
            p = pl.multiple_of(t * 16, 16)
            place = lax.broadcasted_iota(jnp.int32, (16, full), 0) + p
            pick[pl.ds(p, 16), :] = (place == rank).astype(F32).astype(BF)
            return carry

        lax.fori_loop(0, VALID // 16, body, 0)

    x_copy(0).wait()
    compute_r(0)
    pl.semaphore_wait(barrier, nc - 1 + nr - 1)
    start_a(0, 0, send_r, recv_r)

    for d in range(1, nc):
        pltpu.make_async_remote_copy(
            vmine, vrow.at[:, mine], sem_v.at[0], sem_v.at[1],
            device_id={"col": col_peer(d)}, device_id_type=MESH,
        ).start()
    pltpu.make_async_copy(vmine, vrow.at[:, mine], sem_v.at[1]).start()

    def next_r(q):
        x_copy(q).wait()
        compute_r(q)
        start_a(0, q, send_r, recv_r)

    def next_l(q):
        compute_l(q)
        start_a(1, q, send_l, recv_l)

    def loop(low, high, *steps):
        def body(q, carry):
            for step in steps:
                step(q)
            return carry

        lax.fori_loop(low, high, body, 0)

    loop(1, ahead, next_r)

    wait(vrow, sem_v.at[1])
    fill_pick(vrow[...])
    for d in range(1, nr):
        pltpu.make_async_remote_copy(
            vrow, vall.at[row], sem_v.at[2], sem_v.at[3],
            device_id={"row": row_peer(d)}, device_id_type=MESH,
        ).start()
    pltpu.make_async_copy(vrow, vall.at[row], sem_v.at[3]).start()

    def across_r(q):
        compact(0, q, recv_r, put_r)
        send_right(q)

    def across_l(q):
        compact(1, q, recv_l, put_l)
        send_left(q)

    loop(0, nq - ahead, across_r, lambda q: next_r(q + ahead))
    loop(nq - ahead, nq, across_r, lambda q: next_l(q - ahead), lambda q: forward_right(q - ahead))
    loop(0, nq - ahead, across_l, lambda q: next_l(q + ahead), lambda q: forward_right(q + ahead))
    loop(nq - ahead, nq, across_l)

    wait(vall, sem_v.at[3])
    fill_pick(jnp.max(vall[...], axis=0))
    wait(got_r.at[:, :, pl.ds(0, (nr - near + 1) * ti), :], f_recv)

    def pack(t, carry):
        p = pl.multiple_of(t * 256, 256)
        for slot in range(2):
            for n in range(dc):
                packed_r[slot, n, pl.ds(p, 256), :] = dot(pick[pl.ds(p, 256), :], got_r[slot, n]).astype(BF)
        return carry

    lax.fori_loop(0, VALID // 256, pack, 0)

    def product(q):
        wait(got_l.at[q], bl_recv.at[q])
        for slot in range(2):
            for n in range(dc):
                prod[q, slot, n] = dot_t(got_l[q, slot, n], packed_r[slot, n]).astype(BF)
        send_product(q)

    loop(0, nq, product)

    def expand(q):
        part = pl.ds(pl.multiple_of(q * qi, qi), qi)
        wait(send_l.at[pl.ds(0, qi * (nc - 1) // nc)], a_send.at[1, q])
        wait(send_r.at[pl.ds(0, qi * (nc - 1) // nc)], a_send.at[0, q])
        wait(back.at[q], p_recv.at[q])

        def body(t, carry):
            i = pl.multiple_of(q * qi + t * 16, 16)
            a = back[q, :, pl.ds(pl.multiple_of(t * 16, 16), 16), :].reshape(16 * cc, VALID)
            e = dot(dot(perm[...], a).astype(BF), pick[...]).astype(BF)
            for n in range(nc):
                send_l[pl.ds(i, 16), n * cc:(n + 1) * cc, :] = e[:, n * tk:(n + 1) * tk].reshape(16, cc, tk)
            return carry

        lax.fori_loop(0, qi // 16, body, 0)
        dst = field.at[part, pl.ds(pl.multiple_of(col * cc, cc), cc), :]
        for d in range(1, nc):
            to = col_peer(d)
            pltpu.make_async_remote_copy(
                send_l.at[part, pl.ds(pl.multiple_of(to * cc, cc), cc), :], dst,
                e_send.at[q], e_recv.at[q],
                device_id={"col": to}, device_id_type=MESH,
            ).start()
        pltpu.make_async_copy(
            send_l.at[part, pl.ds(pl.multiple_of(col * cc, cc), cc), :], dst, e_recv.at[q]
        ).start()

    def last(q):
        part = pl.ds(pl.multiple_of(q * qi, qi), qi)
        wait(field.at[part], e_recv.at[q])

        def body(t, carry):
            i = q * qi + t * group
            mixed = normalize(lanes(field, i).astype(F32)).astype(BF)
            u = (sigmoid(dot(w_t[4], lanes(normed, i))) * dot(w_t[5], mixed)).astype(BF)
            for h in range(group):
                send_r[i + h] = dot_t(eye[...], u[:, h * tk:(h + 1) * tk]).astype(BF)
            return carry

        lax.fori_loop(0, qi // group, body, 0)
        out_copy(q).start()

    loop(0, lag, expand)
    loop(lag, nq, expand, lambda q: last(q - lag))
    loop(nq - lag, nq, last)

    wait(vrow.at[:, pl.ds(0, full - tk)], sem_v.at[0])
    wait(vall.at[pl.ds(0, nr - 1)], sem_v.at[2])

    def finish(q):
        wait(put_r.at[pl.ds(0, dc * 2 * near), pl.ds(0, qi), :], b_send.at[0, q])
        wait(got_r.at[:, :, pl.ds(0, (near - 1) * qi), :], f_send.at[q])
        wait(put_l.at[pl.ds(0, dc * 2 * (near - 1)), pl.ds(0, qi), :], b_send.at[1, q])
        wait(prod.at[0, :, :, pl.ds(0, (near - 1) * qi), :], p_send.at[q])
        wait(send_l.at[pl.ds(0, qi * (nc - 1) // nc)], e_send.at[q])
        out_copy(q).wait()

    loop(0, nq, finish)


def solution(mesh):
    nr, nc = mesh.shape["row"], mesh.shape["col"]
    nq = 8

    def on_device(pair_rep, pair_mask, w_left_gate, w_left_proj, w_right_gate, w_right_proj, w_gate, w_out):
        ti, tk, cz = pair_rep.shape
        ch = w_left_gate.shape[1]
        cc, dc = ch // nc, ch // nc // nr
        qi = ti // nq
        tile = pltpu.VMEM((ti, ch, tk), BF)
        sem = pltpu.SemaphoreType.DMA
        vmem = pl.BlockSpec(memory_space=pltpu.VMEM)
        return pl.pallas_call(
            functools.partial(kernel, nr, nc, nq),
            out_shape=jax.ShapeDtypeStruct(pair_rep.shape, pair_rep.dtype),
            in_specs=[pl.BlockSpec(memory_space=pl.ANY)] + [vmem] * 7,
            out_specs=pl.BlockSpec(memory_space=pl.ANY),
            scratch_shapes=[
                tile, tile, tile, tile,
                pltpu.VMEM((ti, cc, nc * tk), BF), pltpu.VMEM((ti, cc, nc * tk), BF),
                pltpu.VMEM((cc, ti, VALID), BF), pltpu.VMEM((cc, ti, VALID), BF),
                pltpu.VMEM((2, dc, nr * ti, VALID), BF), pltpu.VMEM((nq, 2, dc, nr // 2 * qi, VALID), BF),
                pltpu.VMEM((2, dc, VALID, VALID), BF),
                pltpu.VMEM((nq, 2, dc, nr // 2 * qi, VALID), BF),
                pltpu.VMEM((nq, cc, qi, VALID), BF),
                pltpu.VMEM((VALID, nc * tk), BF),
                pltpu.VMEM((6, ch, cz), BF),
                pltpu.VMEM((ti, tk), F32), pltpu.VMEM((8, tk), F32),
                pltpu.VMEM((8, nc * tk), F32), pltpu.VMEM((nr, 8, nc * tk), F32),
                pltpu.VMEM((16 * cc, 16 * cc), BF), pltpu.VMEM((ch, ch), BF),
                sem((nq,)), sem((nq,)), sem((4,)), sem((2, nq)), sem((2, nq)), sem((2, nq)),
                sem((nq,)), sem((nq,)), sem(()), sem((nq,)), sem((nq,)), sem((nq,)), sem((nq,)), sem((nq,)),
            ],
            compiler_params=pltpu.CompilerParams(
                collective_id=0, has_side_effects=True, vmem_limit_bytes=58 << 20
            ),
        )(pair_rep, pair_mask, w_left_gate, w_left_proj, w_right_gate, w_right_proj, w_gate, w_out)

    in_specs = (P(("dp", "row"), "col", None), P(("dp", "row"), "col")) + (P(),) * 6
    return jax.shard_map(
        on_device, mesh=mesh, in_specs=in_specs, out_specs=P(("dp", "row"), "col", None), check_vma=False
    )
```

```python
import functools

import jax
import jax.numpy as jnp
from jax import lax
from jax.experimental import pallas as pl
from jax.experimental.pallas import tpu as pltpu
from jax.sharding import PartitionSpec as P

MESH = pl.DeviceIdType.MESH
EPS = 1e-05
VALID = 768
BF = jnp.bfloat16
F32 = jnp.float32


def dot(a, b):
    return jnp.dot(a, b, preferred_element_type=F32)


def dot_t(a, b):
    return lax.dot_general(a, b, (((1,), (1,)), ((), ())), preferred_element_type=F32)


def sigmoid(v):
    return 0.5 * jnp.tanh(0.5 * v) + 0.5


def normalize(v):
    centre = v - jnp.mean(v, axis=0, keepdims=True)
    spread = jnp.mean(centre * centre, axis=0, keepdims=True)
    return centre * lax.rsqrt(spread + EPS)


def wait(ref, sem):
    pltpu.make_async_copy(ref, ref, sem).wait()


def kernel(
    nr, nc, nq,
    x_hbm, mask_ref, wlg_ref, wlp_ref, wrg_ref, wrp_ref, wg_ref, wo_ref,
    out_hbm,
    field, normed, send_r, send_l, recv_r, recv_l, put_r, put_l, got_r, got_l,
    packed_r, prod, back, pick, w_t, maskf, vmine, vrow, vall, perm, eye,
    sem_x, sem_out, sem_v, a_send, a_recv, b_send, br_recv, f_send, f_recv, bl_recv, p_send, p_recv, e_send, e_recv,
):
    row = lax.axis_index("row")
    col = lax.axis_index("col")
    ti, tk = mask_ref.shape
    ch = w_t.shape[1]
    cc = ch // nc
    dc = cc // nr
    qi = ti // nq
    full = nc * tk
    near = nr // 2
    ahead = nq // 2
    lag = 2
    group = 8

    def col_peer(d):
        return lax.rem(col + d, nc)

    def row_peer(d):
        return lax.rem(row + d + nr, nr)

    def x_copy(q):
        part = pl.ds(pl.multiple_of(q * qi, qi), qi)
        return pltpu.make_async_copy(x_hbm.at[part], field.at[part], sem_x.at[q])

    def out_copy(q):
        part = pl.ds(pl.multiple_of(q * qi, qi), qi)
        return pltpu.make_async_copy(send_r.at[part], out_hbm.at[part], sem_out.at[q])

    for q in range(nq):
        x_copy(q).start()

    barrier = pltpu.get_barrier_semaphore()
    for d in range(1, nc):
        pl.semaphore_signal(barrier, inc=1, device_id={"col": col_peer(d)}, device_id_type=MESH)
    for d in range(1, nr):
        pl.semaphore_signal(barrier, inc=1, device_id={"row": row_peer(d)}, device_id_type=MESH)

    eye[...] = (
        lax.broadcasted_iota(jnp.int32, (ch, ch), 0) == lax.broadcasted_iota(jnp.int32, (ch, ch), 1)
    ).astype(F32).astype(BF)
    at = lax.broadcasted_iota(jnp.int32, (cc * qi, cc * qi), 0)
    of = lax.broadcasted_iota(jnp.int32, (cc * qi, cc * qi), 1)
    perm[0] = (of == (at % qi) * cc + at // qi).astype(F32).astype(BF)
    perm[1] = (at == (of % qi) * cc + of // qi).astype(F32).astype(BF)
    for n, ref in enumerate((wrg_ref, wrp_ref, wlg_ref, wlp_ref, wg_ref, wo_ref)):
        w_t[n] = dot_t(eye[...], ref[...]).astype(BF)
    maskf[...] = mask_ref[...].astype(F32)
    vmine[...] = jnp.broadcast_to(jnp.max(maskf[...], axis=0, keepdims=True), vmine.shape)

    mine = pl.ds(pl.multiple_of(col * tk, tk), tk)

    def lanes(ref, i):
        return jnp.concatenate([ref[i + g] for g in range(group)], axis=1)

    def edges(n, vals, i, dst):
        g = dot(w_t[n], vals)
        p = dot(w_t[n + 1], vals)
        m = jnp.concatenate([maskf[pl.ds(i + h, 1), :] for h in range(group)], axis=1)
        e = (sigmoid(g) * p * m).astype(BF)
        for h in range(group):
            dst[i + h] = e[:, h * tk:(h + 1) * tk]

    def compute_r(q):
        def body(t, carry):
            i = q * qi + t * group
            x = field[pl.ds(i, group)].reshape(group * tk, ch)
            vals = normalize(dot_t(eye[...], x)).astype(BF)
            for h in range(group):
                normed[i + h] = vals[:, h * tk:(h + 1) * tk]
            edges(0, vals, i, send_r)
            return carry

        lax.fori_loop(0, qi // group, body, 0)

    def compute_l(q):
        def body(t, carry):
            i = q * qi + t * group
            edges(2, lanes(normed, i), i, send_l)
            return carry

        lax.fori_loop(0, qi // group, body, 0)

    def start_a(n, q, src, dst):
        part = pl.ds(pl.multiple_of(q * qi, qi), qi)
        for d in range(1, nc):
            to = col_peer(d)
            pltpu.make_async_remote_copy(
                src.at[part, pl.ds(pl.multiple_of(to * cc, cc), cc), :], dst.at[part, :, mine],
                a_send.at[n, q], a_recv.at[n, q],
                device_id={"col": to}, device_id_type=MESH,
            ).start()
        pltpu.make_async_copy(
            src.at[part, pl.ds(pl.multiple_of(col * cc, cc), cc), :], dst.at[part, :, mine],
            a_recv.at[n, q],
        ).start()

    def compact(n, q, src, dst):
        part = pl.ds(pl.multiple_of(q * qi, qi), qi)
        wait(src.at[part], a_recv.at[n, q])

        a = src[part].reshape(qi * cc, full)
        b = dot(perm[0], dot_t(a, pick[...]).astype(BF)).astype(BF)
        dst[q] = b.reshape(nr, dc * qi, VALID)

    def start_near(piece, send, recv):
        for b in range(1, near):
            for slot_at, d in ((0, b), (1, -b)):
                src, dst = piece(slot_at, b)
                pltpu.make_async_remote_copy(
                    src, dst, send, recv, device_id={"row": row_peer(d)}, device_id_type=MESH
                ).start()

    def ring(r):
        return lax.rem(r + nr, nr)

    def send_right(q):
        def piece(slot, b):
            group_at = row + b if slot == 0 else row - b - 1
            return put_r.at[q, ring(group_at)], got_r.at[slot, row, q]

        start_near(piece, b_send.at[0, q], br_recv.at[q])
        for slot in range(2):
            src = put_r.at[q, ring(row - slot)]
            pltpu.make_async_remote_copy(
                src, got_r.at[1 - slot, row, q], b_send.at[0, q], f_recv,
                device_id={"row": row_peer(1 - 2 * slot)}, device_id_type=MESH,
            ).start()
            pltpu.make_async_copy(src, got_r.at[slot, row, q], f_recv).start()

    def forward_right(q):
        wait(put_r.at[0, pl.ds(0, 2 * (near - 1))], br_recv.at[q])
        for b in range(1, near):
            for slot in range(2):
                r = ring(row - b if slot == 0 else row + b)
                pltpu.make_async_remote_copy(
                    got_r.at[slot, r, q], got_r.at[1 - slot, r, q], f_send.at[q], f_recv,
                    device_id={"row": row_peer(1 - 2 * slot)}, device_id_type=MESH,
                ).start()

    def send_left(q):
        def piece(slot, b):
            group_at = row + b if slot == 0 else row - b - 1
            return put_l.at[q, ring(group_at)], got_l.at[q, slot, b]

        start_near(piece, b_send.at[1, q], bl_recv.at[q])
        for slot in range(2):
            pltpu.make_async_copy(
                put_l.at[q, ring(row - slot)], got_l.at[q, slot, 0], bl_recv.at[q]
            ).start()

    def send_product(q):
        for b in range(near):
            for slot in range(2):
                src = prod.at[q, slot, b]
                dst = back.at[q, ring(row - slot)]
                if b == 0:
                    pltpu.make_async_copy(src, dst, p_recv.at[q]).start()
                else:
                    pltpu.make_async_remote_copy(
                        src, dst, p_send.at[q], p_recv.at[q],
                        device_id={"row": row_peer(-b if slot == 0 else b)}, device_id_type=MESH,
                    ).start()

    def ranks(v):
        a = lax.broadcasted_iota(jnp.int32, (tk, tk), 0)
        b = lax.broadcasted_iota(jnp.int32, (tk, tk), 1)
        upto = (a <= b).astype(F32).astype(BF)
        ones = jnp.ones((tk, tk), BF)
        base = jnp.zeros((v.shape[0], tk), F32)
        out = []
        for n in range(nc):
            block = v[:, n * tk:(n + 1) * tk]
            block16 = block.astype(BF)
            rank = dot(block16, upto) + base - 1.0
            out.append(jnp.where(block > 0.5, rank, -1.0))
            base = base + dot(block16, ones)
        return jnp.concatenate(out, axis=1)

    def fill_pick(v):
        rank = ranks(v)[0:1, :].astype(jnp.int32)

        def body(t, carry):
            p = pl.multiple_of(t * 16, 16)
            place = lax.broadcasted_iota(jnp.int32, (16, full), 0) + p
            pick[pl.ds(p, 16), :] = (place == rank).astype(F32).astype(BF)
            return carry

        lax.fori_loop(0, VALID // 16, body, 0)

    x_copy(0).wait()
    compute_r(0)
    pl.semaphore_wait(barrier, nc - 1 + nr - 1)
    start_a(0, 0, send_r, recv_r)

    for d in range(1, nc):
        pltpu.make_async_remote_copy(
            vmine, vrow.at[:, mine], sem_v.at[0], sem_v.at[1],
            device_id={"col": col_peer(d)}, device_id_type=MESH,
        ).start()
    pltpu.make_async_copy(vmine, vrow.at[:, mine], sem_v.at[1]).start()

    def next_r(q):
        x_copy(q).wait()
        compute_r(q)
        start_a(0, q, send_r, recv_r)

    def next_l(q):
        compute_l(q)
        start_a(1, q, send_l, recv_l)

    def loop(low, high, *steps):
        def body(q, carry):
            for step in steps:
                step(q)
            return carry

        lax.fori_loop(low, high, body, 0)

    loop(1, ahead, next_r)

    wait(vrow, sem_v.at[1])
    fill_pick(vrow[...])
    for d in range(1, nr):
        pltpu.make_async_remote_copy(
            vrow, vall.at[row], sem_v.at[2], sem_v.at[3],
            device_id={"row": row_peer(d)}, device_id_type=MESH,
        ).start()
    pltpu.make_async_copy(vrow, vall.at[row], sem_v.at[3]).start()

    def across_r(q):
        compact(0, q, recv_r, put_r)
        send_right(q)

    def across_l(q):
        compact(1, q, recv_l, put_l)
        send_left(q)

    loop(0, nq - ahead, across_r, lambda q: next_r(q + ahead))
    loop(nq - ahead, nq, across_r, lambda q: next_l(q - ahead), lambda q: forward_right(q - ahead))
    loop(0, nq - ahead, across_l, lambda q: next_l(q + ahead), lambda q: forward_right(q + ahead))
    loop(nq - ahead, nq, across_l)

    wait(vall, sem_v.at[3])
    fill_pick(jnp.max(vall[...], axis=0))
    wait(got_r.at[:, pl.ds(0, nr - near + 1)], f_recv)
    loop(0, nq, lambda q: wait(put_r.at[0], b_send.at[0, q]))

    blocks = nq // dc
    for slot in range(2):

        def split(r):
            rows = got_r[slot, r].astype(F32).reshape(nq, dc, qi, VALID)
            for n in range(dc):
                put_r[n * blocks + r] = rows[:, n].reshape(ti, VALID).astype(BF).reshape(nr, dc * qi, VALID)

        def pack(t):
            p = pl.multiple_of(t * 256, 256)
            for n in range(dc):
                rows = put_r[n * blocks:(n + 1) * blocks].reshape(nr * ti, VALID)
                packed_r[slot, n, pl.ds(p, 256), :] = dot(pick[pl.ds(p, 256), :], rows).astype(BF)

        loop(0, nr, split)
        loop(0, VALID // 256, pack)

    which = lax.broadcasted_iota(jnp.int32, (near * dc * qi, VALID), 0) // qi % dc

    def product(q):
        wait(got_l.at[q], bl_recv.at[q])
        for slot in range(2):
            rows = got_l[q, slot].reshape(near * dc * qi, VALID)
            out = dot_t(rows, packed_r[slot, 0])
            for n in range(1, dc):
                out = jnp.where(which == n, dot_t(rows, packed_r[slot, n]), out)
            prod[q, slot] = out.astype(BF).reshape(near, dc * qi, VALID)
        send_product(q)

    loop(0, nq, product)

    def expand(q):
        part = pl.ds(pl.multiple_of(q * qi, qi), qi)
        wait(send_l.at[pl.ds(0, qi * (nc - 1) // nc)], a_send.at[1, q])
        wait(send_r.at[pl.ds(0, qi * (nc - 1) // nc)], a_send.at[0, q])
        wait(back.at[q], p_recv.at[q])

        a = back[q].reshape(cc * qi, VALID)
        e = dot(dot(perm[1], a).astype(BF), pick[...]).astype(BF)
        for n in range(nc):
            send_l[part, n * cc:(n + 1) * cc, :] = e[:, n * tk:(n + 1) * tk].reshape(qi, cc, tk)
        dst = field.at[part, pl.ds(pl.multiple_of(col * cc, cc), cc), :]
        for d in range(1, nc):
            to = col_peer(d)
            pltpu.make_async_remote_copy(
                send_l.at[part, pl.ds(pl.multiple_of(to * cc, cc), cc), :], dst,
                e_send.at[q], e_recv.at[q],
                device_id={"col": to}, device_id_type=MESH,
            ).start()
        pltpu.make_async_copy(
            send_l.at[part, pl.ds(pl.multiple_of(col * cc, cc), cc), :], dst, e_recv.at[q]
        ).start()

    def last(q):
        part = pl.ds(pl.multiple_of(q * qi, qi), qi)
        wait(field.at[part], e_recv.at[q])

        def body(t, carry):
            i = q * qi + t * group
            mixed = normalize(lanes(field, i).astype(F32)).astype(BF)
            u = (sigmoid(dot(w_t[4], lanes(normed, i))) * dot(w_t[5], mixed)).astype(BF)
            for h in range(group):
                send_r[i + h] = dot_t(eye[...], u[:, h * tk:(h + 1) * tk]).astype(BF)
            return carry

        lax.fori_loop(0, qi // group, body, 0)
        out_copy(q).start()

    loop(0, lag, expand)
    loop(lag, nq, expand, lambda q: last(q - lag))
    loop(nq - lag, nq, last)

    wait(vrow.at[:, pl.ds(0, full - tk)], sem_v.at[0])
    wait(vall.at[pl.ds(0, nr - 1)], sem_v.at[2])

    def finish(q):
        wait(put_r.at[0, pl.ds(0, 2 * (near - 1))], f_send.at[q])
        wait(put_l.at[0, pl.ds(0, 2 * (near - 1))], b_send.at[1, q])
        wait(prod.at[0, :, pl.ds(0, near - 1)], p_send.at[q])
        wait(send_l.at[pl.ds(0, qi * (nc - 1) // nc)], e_send.at[q])
        out_copy(q).wait()

    loop(0, nq, finish)


def solution(mesh):
    nr, nc = mesh.shape["row"], mesh.shape["col"]
    nq = 16

    def on_device(pair_rep, pair_mask, w_left_gate, w_left_proj, w_right_gate, w_right_proj, w_gate, w_out):
        ti, tk, cz = pair_rep.shape
        ch = w_left_gate.shape[1]
        cc, dc = ch // nc, ch // nc // nr
        qi = ti // nq
        tile = pltpu.VMEM((ti, ch, tk), BF)
        sem = pltpu.SemaphoreType.DMA
        vmem = pl.BlockSpec(memory_space=pltpu.VMEM)
        return pl.pallas_call(
            functools.partial(kernel, nr, nc, nq),
            out_shape=jax.ShapeDtypeStruct(pair_rep.shape, pair_rep.dtype),
            in_specs=[pl.BlockSpec(memory_space=pl.ANY)] + [vmem] * 7,
            out_specs=pl.BlockSpec(memory_space=pl.ANY),
            scratch_shapes=[
                tile, tile, tile, tile,
                pltpu.VMEM((ti, cc, nc * tk), BF), pltpu.VMEM((ti, cc, nc * tk), BF),
                pltpu.VMEM((nq, nr, dc * qi, VALID), BF), pltpu.VMEM((nq, nr, dc * qi, VALID), BF),
                pltpu.VMEM((2, nr, nq, dc * qi, VALID), BF), pltpu.VMEM((nq, 2, nr // 2, dc * qi, VALID), BF),
                pltpu.VMEM((2, dc, VALID, VALID), BF),
                pltpu.VMEM((nq, 2, nr // 2, dc * qi, VALID), BF),
                pltpu.VMEM((nq, nr, dc * qi, VALID), BF),
                pltpu.VMEM((VALID, nc * tk), BF),
                pltpu.VMEM((6, ch, cz), BF),
                pltpu.VMEM((ti, tk), F32), pltpu.VMEM((8, tk), F32),
                pltpu.VMEM((8, nc * tk), F32), pltpu.VMEM((nr, 8, nc * tk), F32),
                pltpu.VMEM((2, qi * cc, qi * cc), BF), pltpu.VMEM((ch, ch), BF),
                sem((nq,)), sem((nq,)), sem((4,)), sem((2, nq)), sem((2, nq)), sem((2, nq)),
                sem((nq,)), sem((nq,)), sem(()), sem((nq,)), sem((nq,)), sem((nq,)), sem((nq,)), sem((nq,)),
            ],
            compiler_params=pltpu.CompilerParams(
                collective_id=0, has_side_effects=True, vmem_limit_bytes=58 << 20
            ),
        )(pair_rep, pair_mask, w_left_gate, w_left_proj, w_right_gate, w_right_proj, w_gate, w_out)

    in_specs = (P(("dp", "row"), "col", None), P(("dp", "row"), "col")) + (P(),) * 6
    return jax.shard_map(
        on_device, mesh=mesh, in_specs=in_specs, out_specs=P(("dp", "row"), "col", None), check_vma=False
    )
```

```python
import functools

import jax
import jax.numpy as jnp
from jax import lax
from jax.experimental import pallas as pl
from jax.experimental.pallas import tpu as pltpu
from jax.sharding import PartitionSpec as P

MESH = pl.DeviceIdType.MESH
EPS = 1e-05
VALID = 768
BF = jnp.bfloat16
F32 = jnp.float32


def dot(a, b):
    return jnp.dot(a, b, preferred_element_type=F32)


def dot_t(a, b):
    return lax.dot_general(a, b, (((1,), (1,)), ((), ())), preferred_element_type=F32)


def sigmoid(v):
    return 0.5 * jnp.tanh(0.5 * v) + 0.5


def normalize(v):
    centre = v - jnp.mean(v, axis=0, keepdims=True)
    spread = jnp.mean(centre * centre, axis=0, keepdims=True)
    return centre * lax.rsqrt(spread + EPS)


def wait(ref, sem):
    pltpu.make_async_copy(ref, ref, sem).wait()


def kernel(
    nr, nc, nq,
    x_hbm, mask_hbm, wlg_hbm, wlp_hbm, wrg_hbm, wrp_hbm, wg_hbm, wo_hbm,
    out_hbm,
    field, normed, send_r, send_l, recv_r, recv_l, put_r, put_l, got_r, got_l,
    packed_r, prod, back, pick, w_in, w_t, mask_in, maskf, vmine, vrow, vall, perm, eye,
    sem_in, sem_x, sem_out, sem_v, a_send, a_recv, b_send, br_recv, f_send, f_recv, bl_recv, p_send, p_recv, e_send, e_recv,
):
    row = lax.axis_index("row")
    col = lax.axis_index("col")
    ti, tk = mask_in.shape
    ch = w_t.shape[1]
    cc = ch // nc
    dc = cc // nr
    qi = ti // nq
    full = nc * tk
    near = nr // 2
    ahead = nq // 4
    behind = nq // 2
    lag = 2
    group = 8

    def col_peer(d):
        return lax.rem(col + d, nc)

    def row_peer(d):
        return lax.rem(row + d + nr, nr)

    def x_copy(q):
        part = pl.ds(pl.multiple_of(q * qi, qi), qi)
        return pltpu.make_async_copy(x_hbm.at[part], field.at[part], sem_x.at[q])

    def out_copy(q):
        part = pl.ds(pl.multiple_of(q * qi, qi), qi)
        return pltpu.make_async_copy(send_r.at[part], out_hbm.at[part], sem_out.at[q])

    barrier = pltpu.get_barrier_semaphore()
    for d in range(1, nc):
        pl.semaphore_signal(barrier, inc=1, device_id={"col": col_peer(d)}, device_id_type=MESH)
    for d in range(1, nr):
        pl.semaphore_signal(barrier, inc=1, device_id={"row": row_peer(d)}, device_id_type=MESH)

    weights = (wrg_hbm, wrp_hbm, wlg_hbm, wlp_hbm, wg_hbm, wo_hbm)
    w_copy = [pltpu.make_async_copy(ref, w_in.at[n], sem_in.at[n]) for n, ref in enumerate(weights)]
    mask_copy = pltpu.make_async_copy(mask_hbm, mask_in, sem_in.at[len(weights)])
    x_copy(0).start()
    for copy in w_copy[:2] + [mask_copy] + w_copy[2:]:
        copy.start()
    for q in range(1, nq):
        x_copy(q).start()

    def turn(n):
        w_copy[n].wait()
        w_t[n] = dot_t(eye[...], w_in[n]).astype(BF)

    eye[...] = (
        lax.broadcasted_iota(jnp.int32, (ch, ch), 0) == lax.broadcasted_iota(jnp.int32, (ch, ch), 1)
    ).astype(F32).astype(BF)
    turn(0)
    turn(1)
    mask_copy.wait()
    maskf[...] = mask_in[...].astype(F32)
    vmine[...] = jnp.broadcast_to(jnp.max(maskf[...], axis=0, keepdims=True), vmine.shape)

    mine = pl.ds(pl.multiple_of(col * tk, tk), tk)

    def lanes(ref, i):
        return jnp.concatenate([ref[i + g] for g in range(group)], axis=1)

    def edges(n, vals, i, dst):
        g = dot(w_t[n], vals)
        p = dot(w_t[n + 1], vals)
        m = jnp.concatenate([maskf[pl.ds(i + h, 1), :] for h in range(group)], axis=1)
        e = (sigmoid(g) * p * m).astype(BF)
        for h in range(group):
            dst[i + h] = e[:, h * tk:(h + 1) * tk]

    def compute_r(q):
        def body(t, carry):
            i = q * qi + t * group
            x = field[pl.ds(i, group)].reshape(group * tk, ch)
            vals = normalize(dot_t(eye[...], x)).astype(BF)
            for h in range(group):
                normed[i + h] = vals[:, h * tk:(h + 1) * tk]
            edges(0, vals, i, send_r)
            return carry

        lax.fori_loop(0, qi // group, body, 0)

    def compute_l(q):
        def body(t, carry):
            i = q * qi + t * group
            edges(2, lanes(normed, i), i, send_l)
            return carry

        lax.fori_loop(0, qi // group, body, 0)

    def start_a(n, q, src, dst):
        part = pl.ds(pl.multiple_of(q * qi, qi), qi)
        for d in range(1, nc):
            to = col_peer(d)
            pltpu.make_async_remote_copy(
                src.at[part, pl.ds(pl.multiple_of(to * cc, cc), cc), :], dst.at[part, :, mine],
                a_send.at[n, q], a_recv.at[n, q],
                device_id={"col": to}, device_id_type=MESH,
            ).start()
        pltpu.make_async_copy(
            src.at[part, pl.ds(pl.multiple_of(col * cc, cc), cc), :], dst.at[part, :, mine],
            a_recv.at[n, q],
        ).start()

    def compact(n, q, src, dst):
        part = pl.ds(pl.multiple_of(q * qi, qi), qi)
        wait(src.at[part], a_recv.at[n, q])

        a = src[part].reshape(qi * cc, full)
        b = dot(perm[0], dot_t(a, pick[...]).astype(BF)).astype(BF)
        dst[q] = b.reshape(nr, dc * qi, VALID)

    def start_near(piece, send, recv):
        for b in range(1, near):
            for slot_at, d in ((0, b), (1, -b)):
                src, dst = piece(slot_at, b)
                pltpu.make_async_remote_copy(
                    src, dst, send, recv, device_id={"row": row_peer(d)}, device_id_type=MESH
                ).start()

    def ring(r):
        return lax.rem(r + nr, nr)

    def send_right(q):
        def piece(slot, b):
            group_at = row + b if slot == 0 else row - b - 1
            return put_r.at[q, ring(group_at)], got_r.at[slot, row, q]

        start_near(piece, b_send.at[0, q], br_recv.at[q])
        for slot in range(2):
            src = put_r.at[q, ring(row - slot)]
            pltpu.make_async_remote_copy(
                src, got_r.at[1 - slot, row, q], b_send.at[0, q], f_recv,
                device_id={"row": row_peer(1 - 2 * slot)}, device_id_type=MESH,
            ).start()
            pltpu.make_async_copy(src, got_r.at[slot, row, q], f_recv).start()

    def forward_right(q):
        wait(put_r.at[0, pl.ds(0, 2 * (near - 1))], br_recv.at[q])
        for b in range(1, near):
            for slot in range(2):
                r = ring(row - b if slot == 0 else row + b)
                pltpu.make_async_remote_copy(
                    got_r.at[slot, r, q], got_r.at[1 - slot, r, q], f_send.at[q], f_recv,
                    device_id={"row": row_peer(1 - 2 * slot)}, device_id_type=MESH,
                ).start()

    def send_left(q):
        def piece(slot, b):
            group_at = row + b if slot == 0 else row - b - 1
            return put_l.at[q, ring(group_at)], got_l.at[q, slot, b]

        start_near(piece, b_send.at[1, q], bl_recv.at[q])
        for slot in range(2):
            pltpu.make_async_copy(
                put_l.at[q, ring(row - slot)], got_l.at[q, slot, 0], bl_recv.at[q]
            ).start()

    def send_product(q):
        for b in range(near):
            for slot in range(2):
                src = prod.at[q, slot, b]
                dst = back.at[q, ring(row - slot)]
                if b == 0:
                    pltpu.make_async_copy(src, dst, p_recv.at[q]).start()
                else:
                    pltpu.make_async_remote_copy(
                        src, dst, p_send.at[q], p_recv.at[q],
                        device_id={"row": row_peer(-b if slot == 0 else b)}, device_id_type=MESH,
                    ).start()

    def ranks(v):
        a = lax.broadcasted_iota(jnp.int32, (tk, tk), 0)
        b = lax.broadcasted_iota(jnp.int32, (tk, tk), 1)
        upto = (a <= b).astype(F32).astype(BF)
        ones = jnp.ones((tk, tk), BF)
        base = jnp.zeros((v.shape[0], tk), F32)
        out = []
        for n in range(nc):
            block = v[:, n * tk:(n + 1) * tk]
            block16 = block.astype(BF)
            rank = dot(block16, upto) + base - 1.0
            out.append(jnp.where(block > 0.5, rank, -1.0))
            base = base + dot(block16, ones)
        return jnp.concatenate(out, axis=1)

    def fill_pick(v):
        rank = ranks(v)[0:1, :].astype(jnp.int32)

        def body(t, carry):
            p = pl.multiple_of(t * 16, 16)
            place = lax.broadcasted_iota(jnp.int32, (16, full), 0) + p
            pick[pl.ds(p, 16), :] = (place == rank).astype(F32).astype(BF)
            return carry

        lax.fori_loop(0, VALID // 16, body, 0)

    x_copy(0).wait()
    compute_r(0)
    pl.semaphore_wait(barrier, nc - 1 + nr - 1)
    start_a(0, 0, send_r, recv_r)

    for d in range(1, nc):
        pltpu.make_async_remote_copy(
            vmine, vrow.at[:, mine], sem_v.at[0], sem_v.at[1],
            device_id={"col": col_peer(d)}, device_id_type=MESH,
        ).start()
    pltpu.make_async_copy(vmine, vrow.at[:, mine], sem_v.at[1]).start()

    for n in range(2, len(weights)):
        turn(n)
    at = lax.broadcasted_iota(jnp.int32, (cc * qi, cc * qi), 0)
    of = lax.broadcasted_iota(jnp.int32, (cc * qi, cc * qi), 1)
    perm[0] = (of == (at % qi) * cc + at // qi).astype(F32).astype(BF)
    perm[1] = (at == (of % qi) * cc + of // qi).astype(F32).astype(BF)

    def next_r(q):
        x_copy(q).wait()
        compute_r(q)
        start_a(0, q, send_r, recv_r)

    def next_l(q):
        compute_l(q)
        start_a(1, q, send_l, recv_l)

    def loop(low, high, *steps):
        def body(q, carry):
            for step in steps:
                step(q)
            return carry

        lax.fori_loop(low, high, body, 0)

    loop(1, ahead, next_r)

    wait(vrow, sem_v.at[1])
    fill_pick(vrow[...])
    for d in range(1, nr):
        pltpu.make_async_remote_copy(
            vrow, vall.at[row], sem_v.at[2], sem_v.at[3],
            device_id={"row": row_peer(d)}, device_id_type=MESH,
        ).start()
    pltpu.make_async_copy(vrow, vall.at[row], sem_v.at[3]).start()

    def across_r(q):
        compact(0, q, recv_r, put_r)
        send_right(q)

    def across_l(q):
        compact(1, q, recv_l, put_l)
        send_left(q)

    edge = nq - ahead
    loop(0, behind, across_r, lambda q: next_r(q + ahead))
    loop(behind, edge, across_r, lambda q: next_r(q + ahead), lambda q: forward_right(q - behind))
    loop(edge, nq, across_r, lambda q: next_l(q - edge), lambda q: forward_right(q - behind))
    loop(0, nq - behind, across_l, lambda q: next_l(q + ahead), lambda q: forward_right(q + behind))
    loop(nq - behind, edge, across_l, lambda q: next_l(q + ahead))
    loop(edge, nq, across_l)

    wait(vall, sem_v.at[3])
    fill_pick(jnp.max(vall[...], axis=0))
    wait(got_r.at[:, pl.ds(0, nr - near + 1)], f_recv)
    loop(0, nq, lambda q: wait(put_r.at[0], b_send.at[0, q]))

    blocks = nq // dc
    for slot in range(2):

        def split(r):
            rows = got_r[slot, r].astype(F32).reshape(nq, dc, qi, VALID)
            for n in range(dc):
                put_r[n * blocks + r] = rows[:, n].reshape(ti, VALID).astype(BF).reshape(nr, dc * qi, VALID)

        def pack(t):
            p = pl.multiple_of(t * 256, 256)
            for n in range(dc):
                rows = put_r[n * blocks:(n + 1) * blocks].reshape(nr * ti, VALID)
                packed_r[slot, n, pl.ds(p, 256), :] = dot(pick[pl.ds(p, 256), :], rows).astype(BF)

        loop(0, nr, split)
        loop(0, VALID // 256, pack)

    which = lax.broadcasted_iota(jnp.int32, (near * dc * qi, VALID), 0) // qi % dc

    def product(q):
        wait(got_l.at[q], bl_recv.at[q])
        for slot in range(2):
            rows = got_l[q, slot].reshape(near * dc * qi, VALID)
            out = dot_t(rows, packed_r[slot, 0])
            for n in range(1, dc):
                out = jnp.where(which == n, dot_t(rows, packed_r[slot, n]), out)
            prod[q, slot] = out.astype(BF).reshape(near, dc * qi, VALID)
        send_product(q)

    loop(0, nq, product)

    def expand(q):
        part = pl.ds(pl.multiple_of(q * qi, qi), qi)
        wait(send_l.at[pl.ds(0, qi * (nc - 1) // nc)], a_send.at[1, q])
        wait(send_r.at[pl.ds(0, qi * (nc - 1) // nc)], a_send.at[0, q])
        wait(back.at[q], p_recv.at[q])

        a = back[q].reshape(cc * qi, VALID)
        e = dot(dot(perm[1], a).astype(BF), pick[...]).astype(BF)
        for n in range(nc):
            send_l[part, n * cc:(n + 1) * cc, :] = e[:, n * tk:(n + 1) * tk].reshape(qi, cc, tk)
        dst = field.at[part, pl.ds(pl.multiple_of(col * cc, cc), cc), :]
        for d in range(1, nc):
            to = col_peer(d)
            pltpu.make_async_remote_copy(
                send_l.at[part, pl.ds(pl.multiple_of(to * cc, cc), cc), :], dst,
                e_send.at[q], e_recv.at[q],
                device_id={"col": to}, device_id_type=MESH,
            ).start()
        pltpu.make_async_copy(
            send_l.at[part, pl.ds(pl.multiple_of(col * cc, cc), cc), :], dst, e_recv.at[q]
        ).start()

    def last(q):
        part = pl.ds(pl.multiple_of(q * qi, qi), qi)
        wait(field.at[part], e_recv.at[q])

        def body(t, carry):
            i = q * qi + t * group
            mixed = normalize(lanes(field, i).astype(F32)).astype(BF)
            u = (sigmoid(dot(w_t[4], lanes(normed, i))) * dot(w_t[5], mixed)).astype(BF)
            for h in range(group):
                send_r[i + h] = dot_t(eye[...], u[:, h * tk:(h + 1) * tk]).astype(BF)
            return carry

        lax.fori_loop(0, qi // group, body, 0)
        out_copy(q).start()

    loop(0, lag, expand)
    loop(lag, nq, expand, lambda q: last(q - lag))
    loop(nq - lag, nq, last)

    wait(vrow.at[:, pl.ds(0, full - tk)], sem_v.at[0])
    wait(vall.at[pl.ds(0, nr - 1)], sem_v.at[2])

    def finish(q):
        wait(put_r.at[0, pl.ds(0, 2 * (near - 1))], f_send.at[q])
        wait(put_l.at[0, pl.ds(0, 2 * (near - 1))], b_send.at[1, q])
        wait(prod.at[0, :, pl.ds(0, near - 1)], p_send.at[q])
        wait(send_l.at[pl.ds(0, qi * (nc - 1) // nc)], e_send.at[q])
        out_copy(q).wait()

    loop(0, nq, finish)


def solution(mesh):
    nr, nc = mesh.shape["row"], mesh.shape["col"]
    nq = 16

    def on_device(pair_rep, pair_mask, w_left_gate, w_left_proj, w_right_gate, w_right_proj, w_gate, w_out):
        ti, tk, cz = pair_rep.shape
        ch = w_left_gate.shape[1]
        cc, dc = ch // nc, ch // nc // nr
        qi = ti // nq
        tile = pltpu.VMEM((ti, ch, tk), BF)
        sem = pltpu.SemaphoreType.DMA
        return pl.pallas_call(
            functools.partial(kernel, nr, nc, nq),
            out_shape=jax.ShapeDtypeStruct(pair_rep.shape, pair_rep.dtype),
            in_specs=[pl.BlockSpec(memory_space=pl.ANY)] * 8,
            out_specs=pl.BlockSpec(memory_space=pl.ANY),
            scratch_shapes=[
                tile, tile, tile, tile,
                pltpu.VMEM((ti, cc, nc * tk), BF), pltpu.VMEM((ti, cc, nc * tk), BF),
                pltpu.VMEM((nq, nr, dc * qi, VALID), BF), pltpu.VMEM((nq, nr, dc * qi, VALID), BF),
                pltpu.VMEM((2, nr, nq, dc * qi, VALID), BF), pltpu.VMEM((nq, 2, nr // 2, dc * qi, VALID), BF),
                pltpu.VMEM((2, dc, VALID, VALID), BF),
                pltpu.VMEM((nq, 2, nr // 2, dc * qi, VALID), BF),
                pltpu.VMEM((nq, nr, dc * qi, VALID), BF),
                pltpu.VMEM((VALID, nc * tk), BF),
                pltpu.VMEM((6, ch, cz), BF), pltpu.VMEM((6, ch, cz), BF),
                pltpu.VMEM((ti, tk), jnp.int32), pltpu.VMEM((ti, tk), F32), pltpu.VMEM((8, tk), F32),
                pltpu.VMEM((8, nc * tk), F32), pltpu.VMEM((nr, 8, nc * tk), F32),
                pltpu.VMEM((2, qi * cc, qi * cc), BF), pltpu.VMEM((ch, ch), BF),
                sem((7,)), sem((nq,)), sem((nq,)), sem((4,)), sem((2, nq)), sem((2, nq)), sem((2, nq)),
                sem((nq,)), sem((nq,)), sem(()), sem((nq,)), sem((nq,)), sem((nq,)), sem((nq,)), sem((nq,)),
            ],
            compiler_params=pltpu.CompilerParams(
                collective_id=0, has_side_effects=True, vmem_limit_bytes=58 << 20
            ),
        )(pair_rep, pair_mask, w_left_gate, w_left_proj, w_right_gate, w_right_proj, w_gate, w_out)

    in_specs = (P(("dp", "row"), "col", None), P(("dp", "row"), "col")) + (P(),) * 6
    return jax.shard_map(
        on_device, mesh=mesh, in_specs=in_specs, out_specs=P(("dp", "row"), "col", None), check_vma=False
    )
```

```python
import functools

import jax
import jax.numpy as jnp
from jax import lax
from jax.experimental import pallas as pl
from jax.experimental.pallas import tpu as pltpu
from jax.sharding import PartitionSpec as P

MESH = pl.DeviceIdType.MESH
EPS = 1e-05
VALID = 768
BF = jnp.bfloat16
F32 = jnp.float32


def dot(a, b):
    return jnp.dot(a, b, preferred_element_type=F32)


def dot_t(a, b):
    return lax.dot_general(a, b, (((1,), (1,)), ((), ())), preferred_element_type=F32)


def sigmoid(v):
    return 0.5 * jnp.tanh(0.5 * v) + 0.5


def normalize(v):
    centre = v - jnp.mean(v, axis=0, keepdims=True)
    spread = jnp.mean(centre * centre, axis=0, keepdims=True)
    return centre * lax.rsqrt(spread + EPS)


def wait(ref, sem):
    pltpu.make_async_copy(ref, ref, sem).wait()


def kernel(
    nr, nc, nq,
    x_hbm, mask_hbm, wlg_hbm, wlp_hbm, wrg_hbm, wrp_hbm, wg_hbm, wo_hbm,
    out_hbm,
    field, normed, send_r, send_l, recv_r, recv_l, put_r, put_l, got_r, got_l,
    packed_r, prod, back, pick, w_in, w_t, mask_in, maskf, vmine, vrow, vall, perm, eye,
    sem_in, sem_x, sem_out, sem_v, a_send, a_recv, b_send, br_recv, f_send, f_recv, bl_recv, p_send, p_recv, e_send, e_recv,
):
    row = lax.axis_index("row")
    col = lax.axis_index("col")
    ti, tk = mask_in.shape
    ch = w_t.shape[1]
    cc = ch // nc
    dc = cc // nr
    qi = ti // nq
    full = nc * tk
    near = nr // 2
    ahead = nq // 4
    behind = nq // 2
    lag = 2
    group = 8

    def col_peer(d):
        return lax.rem(col + d, nc)

    def row_peer(d):
        return lax.rem(row + d + nr, nr)

    def x_copy(q):
        part = pl.ds(pl.multiple_of(q * qi, qi), qi)
        return pltpu.make_async_copy(x_hbm.at[part], field.at[part], sem_x.at[q])

    def out_copy(q):
        part = pl.ds(pl.multiple_of(q * qi, qi), qi)
        return pltpu.make_async_copy(send_r.at[part], out_hbm.at[part], sem_out.at[q])

    barrier = pltpu.get_barrier_semaphore()
    for d in range(1, nc):
        pl.semaphore_signal(barrier, inc=1, device_id={"col": col_peer(d)}, device_id_type=MESH)
    for d in range(1, nr):
        pl.semaphore_signal(barrier, inc=1, device_id={"row": row_peer(d)}, device_id_type=MESH)

    weights = (wrg_hbm, wrp_hbm, wlg_hbm, wlp_hbm, wg_hbm, wo_hbm)
    w_copy = [pltpu.make_async_copy(ref, w_in.at[n], sem_in.at[n]) for n, ref in enumerate(weights)]
    mask_copy = pltpu.make_async_copy(mask_hbm, mask_in, sem_in.at[len(weights)])
    x_copy(0).start()
    for copy in w_copy[:2] + [mask_copy] + w_copy[2:]:
        copy.start()
    for q in range(1, nq):
        x_copy(q).start()

    def turn(n):
        w_copy[n].wait()
        w_t[n] = dot_t(eye[...], w_in[n]).astype(BF)

    eye[...] = (
        lax.broadcasted_iota(jnp.int32, (ch, ch), 0) == lax.broadcasted_iota(jnp.int32, (ch, ch), 1)
    ).astype(F32).astype(BF)
    turn(0)
    turn(1)
    mask_copy.wait()
    maskf[...] = mask_in[...].astype(F32)
    vmine[...] = jnp.broadcast_to(jnp.max(maskf[...], axis=0, keepdims=True), vmine.shape)

    mine = pl.ds(pl.multiple_of(col * tk, tk), tk)

    def lanes(ref, i):
        return jnp.concatenate([ref[i + g] for g in range(group)], axis=1)

    def edges(n, vals, i, dst):
        g = dot(w_t[n], vals)
        p = dot(w_t[n + 1], vals)
        m = jnp.concatenate([maskf[pl.ds(i + h, 1), :] for h in range(group)], axis=1)
        e = (sigmoid(g) * p * m).astype(BF)
        for h in range(group):
            dst[i + h] = e[:, h * tk:(h + 1) * tk]

    def compute_r(q):
        def body(t, carry):
            i = q * qi + t * group
            x = field[pl.ds(i, group)].reshape(group * tk, ch)
            vals = normalize(dot_t(eye[...], x)).astype(BF)
            for h in range(group):
                normed[i + h] = vals[:, h * tk:(h + 1) * tk]
            edges(0, vals, i, send_r)
            return carry

        lax.fori_loop(0, qi // group, body, 0)

    def compute_l(q):
        def body(t, carry):
            i = q * qi + t * group
            edges(2, lanes(normed, i), i, send_l)
            return carry

        lax.fori_loop(0, qi // group, body, 0)

    def start_a(n, q, src, dst):
        part = pl.ds(pl.multiple_of(q * qi, qi), qi)
        for d in range(1, nc):
            to = col_peer(d)
            pltpu.make_async_remote_copy(
                src.at[part, pl.ds(pl.multiple_of(to * cc, cc), cc), :], dst.at[part, :, mine],
                a_send.at[n, q], a_recv.at[n, q],
                device_id={"col": to}, device_id_type=MESH,
            ).start()
        pltpu.make_async_copy(
            src.at[part, pl.ds(pl.multiple_of(col * cc, cc), cc), :], dst.at[part, :, mine],
            a_recv.at[n, q],
        ).start()

    def compact(n, q, src, dst):
        part = pl.ds(pl.multiple_of(q * qi, qi), qi)
        wait(src.at[part], a_recv.at[n, q])

        a = src[part].reshape(qi * cc, full)
        b = dot(perm[0], dot_t(a, pick[...]).astype(BF)).astype(BF)
        dst[q] = b.reshape(nr, dc * qi, VALID)

    def start_near(piece, send, recv):
        for b in range(1, near):
            for slot_at, d in ((0, b), (1, -b)):
                src, dst = piece(slot_at, b)
                pltpu.make_async_remote_copy(
                    src, dst, send, recv, device_id={"row": row_peer(d)}, device_id_type=MESH
                ).start()

    def ring(r):
        return lax.rem(r + nr, nr)

    def send_right(q):
        def piece(slot, b):
            group_at = row + b if slot == 0 else row - b - 1
            return put_r.at[q, ring(group_at)], got_r.at[slot, row, q]

        start_near(piece, b_send.at[0, q], br_recv.at[q])
        for slot in range(2):
            src = put_r.at[q, ring(row - slot)]
            pltpu.make_async_remote_copy(
                src, got_r.at[1 - slot, row, q], b_send.at[0, q], f_recv,
                device_id={"row": row_peer(1 - 2 * slot)}, device_id_type=MESH,
            ).start()
            pltpu.make_async_copy(src, got_r.at[slot, row, q], f_recv).start()

    def forward_right(q):
        wait(put_r.at[0, pl.ds(0, 2 * (near - 1))], br_recv.at[q])
        for b in range(1, near):
            for slot in range(2):
                r = ring(row - b if slot == 0 else row + b)
                pltpu.make_async_remote_copy(
                    got_r.at[slot, r, q], got_r.at[1 - slot, r, q], f_send.at[q], f_recv,
                    device_id={"row": row_peer(1 - 2 * slot)}, device_id_type=MESH,
                ).start()

    def send_left(q):
        def piece(slot, b):
            group_at = row + b if slot == 0 else row - b - 1
            return put_l.at[q, ring(group_at)], got_l.at[q, slot, b]

        start_near(piece, b_send.at[1, q], bl_recv.at[q])
        for slot in range(2):
            pltpu.make_async_copy(
                put_l.at[q, ring(row - slot)], got_l.at[q, slot, 0], bl_recv.at[q]
            ).start()

    def send_product(q):
        for b in range(near):
            for slot in range(2):
                src = prod.at[q, slot, b]
                dst = back.at[q, ring(row - slot)]
                if b == 0:
                    pltpu.make_async_copy(src, dst, p_recv.at[q]).start()
                else:
                    pltpu.make_async_remote_copy(
                        src, dst, p_send.at[q], p_recv.at[q],
                        device_id={"row": row_peer(-b if slot == 0 else b)}, device_id_type=MESH,
                    ).start()

    def ranks(v):
        a = lax.broadcasted_iota(jnp.int32, (tk, tk), 0)
        b = lax.broadcasted_iota(jnp.int32, (tk, tk), 1)
        upto = (a <= b).astype(F32).astype(BF)
        ones = jnp.ones((tk, tk), BF)
        base = jnp.zeros((v.shape[0], tk), F32)
        out = []
        for n in range(nc):
            block = v[:, n * tk:(n + 1) * tk]
            block16 = block.astype(BF)
            rank = dot(block16, upto) + base - 1.0
            out.append(jnp.where(block > 0.5, rank, -1.0))
            base = base + dot(block16, ones)
        return jnp.concatenate(out, axis=1)

    def fill_pick(v):
        rank = ranks(v)[0:1, :].astype(jnp.int32)

        def body(t, carry):
            p = pl.multiple_of(t * 16, 16)
            place = lax.broadcasted_iota(jnp.int32, (16, full), 0) + p
            pick[pl.ds(p, 16), :] = (place == rank).astype(F32).astype(BF)
            return carry

        lax.fori_loop(0, VALID // 16, body, 0)

    x_copy(0).wait()
    compute_r(0)
    pl.semaphore_wait(barrier, nc - 1 + nr - 1)
    for d in range(1, nc):
        pltpu.make_async_remote_copy(
            vmine, vrow.at[:, mine], sem_v.at[0], sem_v.at[1],
            device_id={"col": col_peer(d)}, device_id_type=MESH,
        ).start()
    pltpu.make_async_copy(vmine, vrow.at[:, mine], sem_v.at[1]).start()

    start_a(0, 0, send_r, recv_r)

    for n in range(2, len(weights)):
        turn(n)
    at = lax.broadcasted_iota(jnp.int32, (cc * qi, cc * qi), 0)
    of = lax.broadcasted_iota(jnp.int32, (cc * qi, cc * qi), 1)
    perm[0] = (of == (at % qi) * cc + at // qi).astype(F32).astype(BF)
    perm[1] = (at == (of % qi) * cc + of // qi).astype(F32).astype(BF)

    def next_r(q):
        x_copy(q).wait()
        compute_r(q)
        start_a(0, q, send_r, recv_r)

    def next_l(q):
        compute_l(q)
        start_a(1, q, send_l, recv_l)

    def loop(low, high, *steps):
        def body(q, carry):
            for step in steps:
                step(q)
            return carry

        lax.fori_loop(low, high, body, 0)

    loop(1, ahead, next_r)

    wait(vrow, sem_v.at[1])
    fill_pick(vrow[...])
    for d in range(1, nr):
        pltpu.make_async_remote_copy(
            vrow, vall.at[row], sem_v.at[2], sem_v.at[3],
            device_id={"row": row_peer(d)}, device_id_type=MESH,
        ).start()
    pltpu.make_async_copy(vrow, vall.at[row], sem_v.at[3]).start()

    def across_r(q):
        compact(0, q, recv_r, put_r)
        send_right(q)

    def across_l(q):
        compact(1, q, recv_l, put_l)
        send_left(q)

    edge = nq - ahead
    loop(0, behind, across_r, lambda q: next_r(q + ahead))
    loop(behind, edge, across_r, lambda q: next_r(q + ahead), lambda q: forward_right(q - behind))
    loop(edge, nq, across_r, lambda q: next_l(q - edge), lambda q: forward_right(q - behind))
    loop(0, nq - behind, across_l, lambda q: next_l(q + ahead), lambda q: forward_right(q + behind))
    loop(nq - behind, edge, across_l, lambda q: next_l(q + ahead))
    loop(edge, nq, across_l)

    wait(vall, sem_v.at[3])
    fill_pick(jnp.max(vall[...], axis=0))
    wait(got_r.at[:, pl.ds(0, nr - near + 1)], f_recv)
    loop(0, nq, lambda q: wait(put_r.at[0], b_send.at[0, q]))

    blocks = nq // dc
    for slot in range(2):

        def split(r):
            rows = got_r[slot, r].astype(F32).reshape(nq, dc, qi, VALID)
            for n in range(dc):
                put_r[n * blocks + r] = rows[:, n].reshape(ti, VALID).astype(BF).reshape(nr, dc * qi, VALID)

        def pack(t):
            p = pl.multiple_of(t * 256, 256)
            for n in range(dc):
                rows = put_r[n * blocks:(n + 1) * blocks].reshape(nr * ti, VALID)
                packed_r[slot, n, pl.ds(p, 256), :] = dot(pick[pl.ds(p, 256), :], rows).astype(BF)

        loop(0, nr, split)
        loop(0, VALID // 256, pack)

    which = lax.broadcasted_iota(jnp.int32, (near * dc * qi, VALID), 0) // qi % dc

    def product(q):
        wait(got_l.at[q], bl_recv.at[q])
        for slot in range(2):
            rows = got_l[q, slot].reshape(near * dc * qi, VALID)
            out = dot_t(rows, packed_r[slot, 0])
            for n in range(1, dc):
                out = jnp.where(which == n, dot_t(rows, packed_r[slot, n]), out)
            prod[q, slot] = out.astype(BF).reshape(near, dc * qi, VALID)
        send_product(q)

    loop(0, nq, product)

    def expand(q):
        part = pl.ds(pl.multiple_of(q * qi, qi), qi)
        wait(send_l.at[pl.ds(0, qi * (nc - 1) // nc)], a_send.at[1, q])
        wait(send_r.at[pl.ds(0, qi * (nc - 1) // nc)], a_send.at[0, q])
        wait(back.at[q], p_recv.at[q])

        a = back[q].reshape(cc * qi, VALID)
        e = dot(dot(perm[1], a).astype(BF), pick[...]).astype(BF)
        for n in range(nc):
            send_l[part, n * cc:(n + 1) * cc, :] = e[:, n * tk:(n + 1) * tk].reshape(qi, cc, tk)
        dst = field.at[part, pl.ds(pl.multiple_of(col * cc, cc), cc), :]
        for d in range(1, nc):
            to = col_peer(d)
            pltpu.make_async_remote_copy(
                send_l.at[part, pl.ds(pl.multiple_of(to * cc, cc), cc), :], dst,
                e_send.at[q], e_recv.at[q],
                device_id={"col": to}, device_id_type=MESH,
            ).start()
        pltpu.make_async_copy(
            send_l.at[part, pl.ds(pl.multiple_of(col * cc, cc), cc), :], dst, e_recv.at[q]
        ).start()

    def last(q):
        part = pl.ds(pl.multiple_of(q * qi, qi), qi)
        wait(field.at[part], e_recv.at[q])

        def body(t, carry):
            i = q * qi + t * group
            mixed = normalize(lanes(field, i).astype(F32)).astype(BF)
            u = (sigmoid(dot(w_t[4], lanes(normed, i))) * dot(w_t[5], mixed)).astype(BF)
            for h in range(group):
                send_r[i + h] = dot_t(eye[...], u[:, h * tk:(h + 1) * tk]).astype(BF)
            return carry

        lax.fori_loop(0, qi // group, body, 0)
        out_copy(q).start()

    loop(0, lag, expand)
    loop(lag, nq, expand, lambda q: last(q - lag))
    loop(nq - lag, nq, last)

    wait(vrow.at[:, pl.ds(0, full - tk)], sem_v.at[0])
    wait(vall.at[pl.ds(0, nr - 1)], sem_v.at[2])

    def finish(q):
        wait(put_r.at[0, pl.ds(0, 2 * (near - 1))], f_send.at[q])
        wait(put_l.at[0, pl.ds(0, 2 * (near - 1))], b_send.at[1, q])
        wait(prod.at[0, :, pl.ds(0, near - 1)], p_send.at[q])
        wait(send_l.at[pl.ds(0, qi * (nc - 1) // nc)], e_send.at[q])
        out_copy(q).wait()

    loop(0, nq, finish)


def hand_over(src, dst, held, sem_in, sem_out):
    parts = sem_in.shape[0]
    size = src.shape[0] // parts
    pieces = [pl.ds(n * size, size) for n in range(parts)]
    reads = [pltpu.make_async_copy(src.at[p], held.at[p], sem_in.at[n]) for n, p in enumerate(pieces)]
    writes = [pltpu.make_async_copy(held.at[p], dst.at[p], sem_out.at[n]) for n, p in enumerate(pieces)]
    for read in reads:
        read.start()
    for read, write in zip(reads, writes):
        read.wait()
        write.start()
    for write in writes:
        write.wait()


def solution(mesh):
    nr, nc = mesh.shape["row"], mesh.shape["col"]
    nq = 16

    def on_device(pair_rep, pair_mask, w_left_gate, w_left_proj, w_right_gate, w_right_proj, w_gate, w_out):
        ti, tk, cz = pair_rep.shape
        ch = w_left_gate.shape[1]
        cc, dc = ch // nc, ch // nc // nr
        qi = ti // nq
        tile = pltpu.VMEM((ti, ch, tk), BF)
        sem = pltpu.SemaphoreType.DMA
        update = pl.pallas_call(
            functools.partial(kernel, nr, nc, nq),
            out_shape=jax.ShapeDtypeStruct(pair_rep.shape, pair_rep.dtype),
            in_specs=[pl.BlockSpec(memory_space=pl.ANY)] * 8,
            out_specs=pl.BlockSpec(memory_space=pl.ANY),
            scratch_shapes=[
                tile, tile, tile, tile,
                pltpu.VMEM((ti, cc, nc * tk), BF), pltpu.VMEM((ti, cc, nc * tk), BF),
                pltpu.VMEM((nq, nr, dc * qi, VALID), BF), pltpu.VMEM((nq, nr, dc * qi, VALID), BF),
                pltpu.VMEM((2, nr, nq, dc * qi, VALID), BF), pltpu.VMEM((nq, 2, nr // 2, dc * qi, VALID), BF),
                pltpu.VMEM((2, dc, VALID, VALID), BF),
                pltpu.VMEM((nq, 2, nr // 2, dc * qi, VALID), BF),
                pltpu.VMEM((nq, nr, dc * qi, VALID), BF),
                pltpu.VMEM((VALID, nc * tk), BF),
                pltpu.VMEM((6, ch, cz), BF), pltpu.VMEM((6, ch, cz), BF),
                pltpu.VMEM((ti, tk), jnp.int32), pltpu.VMEM((ti, tk), F32), pltpu.VMEM((8, tk), F32),
                pltpu.VMEM((8, nc * tk), F32), pltpu.VMEM((nr, 8, nc * tk), F32),
                pltpu.VMEM((2, qi * cc, qi * cc), BF), pltpu.VMEM((ch, ch), BF),
                sem((7,)), sem((nq,)), sem((nq,)), sem((4,)), sem((2, nq)), sem((2, nq)), sem((2, nq)),
                sem((nq,)), sem((nq,)), sem(()), sem((nq,)), sem((nq,)), sem((nq,)), sem((nq,)), sem((nq,)),
            ],
            compiler_params=pltpu.CompilerParams(
                collective_id=0, has_side_effects=True, vmem_limit_bytes=58 << 20
            ),
        )(pair_rep, pair_mask, w_left_gate, w_left_proj, w_right_gate, w_right_proj, w_gate, w_out)
        return pl.pallas_call(
            hand_over,
            out_shape=jax.ShapeDtypeStruct(pair_rep.shape, pair_rep.dtype),
            in_specs=[pl.BlockSpec(memory_space=pl.ANY)],
            out_specs=pl.BlockSpec(memory_space=pl.ANY),
            scratch_shapes=[pltpu.VMEM(pair_rep.shape, pair_rep.dtype), sem((8,)), sem((8,))],
            compiler_params=pltpu.CompilerParams(vmem_limit_bytes=56 << 20),
        )(update)

    in_specs = (P(("dp", "row"), "col", None), P(("dp", "row"), "col")) + (P(),) * 6
    return jax.shard_map(
        on_device, mesh=mesh, in_specs=in_specs, out_specs=P(("dp", "row"), "col", None), check_vma=False
    )
```

```python
import functools

import jax
import jax.numpy as jnp
from jax import lax
from jax.experimental import pallas as pl
from jax.experimental.pallas import tpu as pltpu
from jax.sharding import PartitionSpec as P

MESH = pl.DeviceIdType.MESH
EPS = 1e-05
VALID = 768
BF = jnp.bfloat16
F32 = jnp.float32


def dot(a, b):
    return jnp.dot(a, b, preferred_element_type=F32)


def dot_t(a, b):
    return lax.dot_general(a, b, (((1,), (1,)), ((), ())), preferred_element_type=F32)


def sigmoid(v):
    return 0.5 * jnp.tanh(0.5 * v) + 0.5


def normalize(v):
    centre = v - jnp.mean(v, axis=0, keepdims=True)
    spread = jnp.mean(centre * centre, axis=0, keepdims=True)
    return centre * lax.rsqrt(spread + EPS)


def wait(ref, sem):
    pltpu.make_async_copy(ref, ref, sem).wait()


def kernel(
    nr, nc, nq,
    x_hbm, mask_hbm, wlg_hbm, wlp_hbm, wrg_hbm, wrp_hbm, wg_hbm, wo_hbm,
    out_hbm,
    field, normed, send_r, send_l, recv_r, recv_l, put_r, put_l, got_r, got_l,
    packed_r, prod, back, pick, w_in, w_t, mask_in, maskf, vmine, vrow, vpack, vall, perm, eye,
    sem_in, sem_x, sem_out, sem_v, a_send, a_recv, b_send, br_recv, f_send, f_recv, bl_recv, p_send, p_recv, e_send, e_recv,
):
    row = lax.axis_index("row")
    col = lax.axis_index("col")
    ti, tk = mask_in.shape
    ch = w_t.shape[1]
    cc = ch // nc
    dc = cc // nr
    qi = ti // nq
    full = nc * tk
    near = nr // 2
    ahead = nq // 4
    behind = nq // 2
    lag = 2
    group = 8

    def col_peer(d):
        return lax.rem(col + d, nc)

    def row_peer(d):
        return lax.rem(row + d + nr, nr)

    def x_copy(q):
        part = pl.ds(pl.multiple_of(q * qi, qi), qi)
        return pltpu.make_async_copy(x_hbm.at[part], field.at[part], sem_x.at[q])

    def out_copy(q):
        part = pl.ds(pl.multiple_of(q * qi, qi), qi)
        return pltpu.make_async_copy(send_r.at[part], out_hbm.at[part], sem_out.at[q])

    barrier = pltpu.get_barrier_semaphore()
    for d in range(1, nc):
        pl.semaphore_signal(barrier, inc=1, device_id={"col": col_peer(d)}, device_id_type=MESH)
    for d in range(1, nr):
        pl.semaphore_signal(barrier, inc=1, device_id={"row": row_peer(d)}, device_id_type=MESH)

    weights = (wrg_hbm, wrp_hbm, wlg_hbm, wlp_hbm, wg_hbm, wo_hbm)
    w_copy = [pltpu.make_async_copy(ref, w_in.at[n], sem_in.at[n]) for n, ref in enumerate(weights)]
    mask_copy = pltpu.make_async_copy(mask_hbm, mask_in, sem_in.at[len(weights)])
    x_copy(0).start()
    for copy in w_copy[:2] + [mask_copy] + w_copy[2:]:
        copy.start()
    for q in range(1, nq):
        x_copy(q).start()

    def turn(n):
        w_copy[n].wait()
        w_t[n] = dot_t(eye[...], w_in[n]).astype(BF)

    eye[...] = (
        lax.broadcasted_iota(jnp.int32, (ch, ch), 0) == lax.broadcasted_iota(jnp.int32, (ch, ch), 1)
    ).astype(F32).astype(BF)
    turn(0)
    turn(1)
    mask_copy.wait()
    maskf[...] = mask_in[...].astype(F32)
    vmine[...] = jnp.broadcast_to(jnp.max(maskf[...], axis=0, keepdims=True), vmine.shape)

    mine = pl.ds(pl.multiple_of(col * tk, tk), tk)

    def lanes(ref, i):
        return jnp.concatenate([ref[i + g] for g in range(group)], axis=1)

    def edges(n, vals, i, dst):
        g = dot(w_t[n], vals)
        p = dot(w_t[n + 1], vals)
        m = jnp.concatenate([maskf[pl.ds(i + h, 1), :] for h in range(group)], axis=1)
        e = (sigmoid(g) * p * m).astype(BF)
        for h in range(group):
            dst[i + h] = e[:, h * tk:(h + 1) * tk]

    def compute_r(q):
        def body(t, carry):
            i = q * qi + t * group
            x = field[pl.ds(i, group)].reshape(group * tk, ch)
            vals = normalize(dot_t(eye[...], x)).astype(BF)
            for h in range(group):
                normed[i + h] = vals[:, h * tk:(h + 1) * tk]
            edges(0, vals, i, send_r)
            return carry

        lax.fori_loop(0, qi // group, body, 0)

    def compute_l(q):
        def body(t, carry):
            i = q * qi + t * group
            edges(2, lanes(normed, i), i, send_l)
            return carry

        lax.fori_loop(0, qi // group, body, 0)

    def start_a(n, q, src, dst):
        part = pl.ds(pl.multiple_of(q * qi, qi), qi)
        for d in range(1, nc):
            to = col_peer(d)
            pltpu.make_async_remote_copy(
                src.at[part, pl.ds(pl.multiple_of(to * cc, cc), cc), :], dst.at[part, :, mine],
                a_send.at[n, q], a_recv.at[n, q],
                device_id={"col": to}, device_id_type=MESH,
            ).start()
        pltpu.make_async_copy(
            src.at[part, pl.ds(pl.multiple_of(col * cc, cc), cc), :], dst.at[part, :, mine],
            a_recv.at[n, q],
        ).start()

    def compact(n, q, src, dst):
        part = pl.ds(pl.multiple_of(q * qi, qi), qi)
        wait(src.at[part], a_recv.at[n, q])

        a = src[part].reshape(qi * cc, full)
        b = dot(perm[0], dot_t(a, pick[...]).astype(BF)).astype(BF)
        dst[q] = b.reshape(nr, dc * qi, VALID)

    def start_near(piece, send, recv):
        for b in range(1, near):
            for slot_at, d in ((0, b), (1, -b)):
                src, dst = piece(slot_at, b)
                pltpu.make_async_remote_copy(
                    src, dst, send, recv, device_id={"row": row_peer(d)}, device_id_type=MESH
                ).start()

    def ring(r):
        return lax.rem(r + nr, nr)

    def send_right(q):
        def piece(slot, b):
            group_at = row + b if slot == 0 else row - b - 1
            return put_r.at[q, ring(group_at)], got_r.at[slot, row, q]

        start_near(piece, b_send.at[0, q], br_recv.at[q])
        for slot in range(2):
            src = put_r.at[q, ring(row - slot)]
            pltpu.make_async_remote_copy(
                src, got_r.at[1 - slot, row, q], b_send.at[0, q], f_recv,
                device_id={"row": row_peer(1 - 2 * slot)}, device_id_type=MESH,
            ).start()
            pltpu.make_async_copy(src, got_r.at[slot, row, q], f_recv).start()

    def forward_right(q):
        wait(put_r.at[0, pl.ds(0, 2 * (near - 1))], br_recv.at[q])
        for b in range(1, near):
            for slot in range(2):
                r = ring(row - b if slot == 0 else row + b)
                pltpu.make_async_remote_copy(
                    got_r.at[slot, r, q], got_r.at[1 - slot, r, q], f_send.at[q], f_recv,
                    device_id={"row": row_peer(1 - 2 * slot)}, device_id_type=MESH,
                ).start()

    def send_left(q):
        def piece(slot, b):
            group_at = row + b if slot == 0 else row - b - 1
            return put_l.at[q, ring(group_at)], got_l.at[q, slot, b]

        start_near(piece, b_send.at[1, q], bl_recv.at[q])
        for slot in range(2):
            pltpu.make_async_copy(
                put_l.at[q, ring(row - slot)], got_l.at[q, slot, 0], bl_recv.at[q]
            ).start()

    def send_product(q):
        for b in range(near):
            for slot in range(2):
                src = prod.at[q, slot, b]
                dst = back.at[q, ring(row - slot)]
                if b == 0:
                    pltpu.make_async_copy(src, dst, p_recv.at[q]).start()
                else:
                    pltpu.make_async_remote_copy(
                        src, dst, p_send.at[q], p_recv.at[q],
                        device_id={"row": row_peer(-b if slot == 0 else b)}, device_id_type=MESH,
                    ).start()

    def ranks(v):
        a = lax.broadcasted_iota(jnp.int32, (tk, tk), 0)
        b = lax.broadcasted_iota(jnp.int32, (tk, tk), 1)
        upto = (a <= b).astype(F32).astype(BF)
        ones = jnp.ones((tk, tk), BF)
        base = jnp.zeros((v.shape[0], tk), F32)
        out = []
        for n in range(nc):
            block = v[:, n * tk:(n + 1) * tk]
            block16 = block.astype(BF)
            rank = dot(block16, upto) + base - 1.0
            out.append(jnp.where(block > 0.5, rank, -1.0))
            base = base + dot(block16, ones)
        return jnp.concatenate(out, axis=1)

    def fill_pick(v):
        rank = ranks(v)[0:1, :].astype(jnp.int32)

        def body(t, carry):
            p = pl.multiple_of(t * 16, 16)
            place = lax.broadcasted_iota(jnp.int32, (16, full), 0) + p
            pick[pl.ds(p, 16), :] = (place == rank).astype(F32).astype(BF)
            return carry

        lax.fori_loop(0, VALID // 16, body, 0)

    x_copy(0).wait()
    compute_r(0)
    pl.semaphore_wait(barrier, nc - 1 + nr - 1)
    for d in range(1, nc):
        pltpu.make_async_remote_copy(
            vmine, vrow.at[:, mine], sem_v.at[0], sem_v.at[1],
            device_id={"col": col_peer(d)}, device_id_type=MESH,
        ).start()
    pltpu.make_async_copy(vmine, vrow.at[:, mine], sem_v.at[1]).start()

    start_a(0, 0, send_r, recv_r)

    for n in range(2, len(weights)):
        turn(n)
    at = lax.broadcasted_iota(jnp.int32, (cc * qi, cc * qi), 0)
    of = lax.broadcasted_iota(jnp.int32, (cc * qi, cc * qi), 1)
    perm[0] = (of == (at % qi) * cc + at // qi).astype(F32).astype(BF)
    perm[1] = (at == (of % qi) * cc + of // qi).astype(F32).astype(BF)

    def next_r(q):
        x_copy(q).wait()
        compute_r(q)
        start_a(0, q, send_r, recv_r)

    def next_l(q):
        compute_l(q)
        start_a(1, q, send_l, recv_l)

    def loop(low, high, *steps):
        def body(q, carry):
            for step in steps:
                step(q)
            return carry

        lax.fori_loop(low, high, body, 0)

    loop(1, ahead, next_r)

    wait(vrow, sem_v.at[1])
    for n in range(nc):
        vpack[n:n + 1, :] = vrow[0:1, n * tk:(n + 1) * tk]
    for d in range(1, nr):
        pltpu.make_async_remote_copy(
            vpack, vall.at[row], sem_v.at[2], sem_v.at[3],
            device_id={"row": row_peer(d)}, device_id_type=MESH,
        ).start()
    pltpu.make_async_copy(vpack, vall.at[row], sem_v.at[3]).start()
    fill_pick(vrow[...])

    def across_r(q):
        compact(0, q, recv_r, put_r)
        send_right(q)

    def across_l(q):
        compact(1, q, recv_l, put_l)
        send_left(q)

    edge = nq - ahead
    loop(0, behind, across_r, lambda q: next_r(q + ahead))
    loop(behind, edge, across_r, lambda q: next_r(q + ahead), lambda q: forward_right(q - behind))
    loop(edge, nq, across_r, lambda q: next_l(q - edge), lambda q: forward_right(q - behind))
    loop(0, nq - behind, across_l, lambda q: next_l(q + ahead), lambda q: forward_right(q + behind))
    loop(nq - behind, edge, across_l, lambda q: next_l(q + ahead))
    loop(edge, nq, across_l)

    wait(vall, sem_v.at[3])
    valid = jnp.max(vall[...], axis=0)
    fill_pick(jnp.concatenate([jnp.broadcast_to(valid[n:n + 1, :], vmine.shape) for n in range(nc)], axis=1))
    wait(got_r.at[:, pl.ds(0, nr - near + 1)], f_recv)
    loop(0, nq, lambda q: wait(put_r.at[0], b_send.at[0, q]))

    blocks = nq // dc
    for slot in range(2):

        def split(r):
            rows = got_r[slot, r].astype(F32).reshape(nq, dc, qi, VALID)
            for n in range(dc):
                put_r[n * blocks + r] = rows[:, n].reshape(ti, VALID).astype(BF).reshape(nr, dc * qi, VALID)

        def pack(t):
            p = pl.multiple_of(t * 256, 256)
            for n in range(dc):
                rows = put_r[n * blocks:(n + 1) * blocks].reshape(nr * ti, VALID)
                packed_r[slot, n, pl.ds(p, 256), :] = dot(pick[pl.ds(p, 256), :], rows).astype(BF)

        loop(0, nr, split)
        loop(0, VALID // 256, pack)

    which = lax.broadcasted_iota(jnp.int32, (near * dc * qi, VALID), 0) // qi % dc

    def product(q):
        wait(got_l.at[q], bl_recv.at[q])
        for slot in range(2):
            rows = got_l[q, slot].reshape(near * dc * qi, VALID)
            out = dot_t(rows, packed_r[slot, 0])
            for n in range(1, dc):
                out = jnp.where(which == n, dot_t(rows, packed_r[slot, n]), out)
            prod[q, slot] = out.astype(BF).reshape(near, dc * qi, VALID)
        send_product(q)

    loop(0, nq, product)

    def expand(q):
        part = pl.ds(pl.multiple_of(q * qi, qi), qi)
        wait(send_l.at[pl.ds(0, qi * (nc - 1) // nc)], a_send.at[1, q])
        wait(send_r.at[pl.ds(0, qi * (nc - 1) // nc)], a_send.at[0, q])
        wait(back.at[q], p_recv.at[q])

        a = back[q].reshape(cc * qi, VALID)
        e = dot(dot(perm[1], a).astype(BF), pick[...]).astype(BF)
        for n in range(nc):
            send_l[part, n * cc:(n + 1) * cc, :] = e[:, n * tk:(n + 1) * tk].reshape(qi, cc, tk)
        dst = field.at[part, pl.ds(pl.multiple_of(col * cc, cc), cc), :]
        for d in range(1, nc):
            to = col_peer(d)
            pltpu.make_async_remote_copy(
                send_l.at[part, pl.ds(pl.multiple_of(to * cc, cc), cc), :], dst,
                e_send.at[q], e_recv.at[q],
                device_id={"col": to}, device_id_type=MESH,
            ).start()
        pltpu.make_async_copy(
            send_l.at[part, pl.ds(pl.multiple_of(col * cc, cc), cc), :], dst, e_recv.at[q]
        ).start()

    def last(q):
        part = pl.ds(pl.multiple_of(q * qi, qi), qi)
        wait(field.at[part], e_recv.at[q])

        def body(t, carry):
            i = q * qi + t * group
            mixed = normalize(lanes(field, i).astype(F32)).astype(BF)
            u = (sigmoid(dot(w_t[4], lanes(normed, i))) * dot(w_t[5], mixed)).astype(BF)
            for h in range(group):
                send_r[i + h] = dot_t(eye[...], u[:, h * tk:(h + 1) * tk]).astype(BF)
            return carry

        lax.fori_loop(0, qi // group, body, 0)
        out_copy(q).start()

    loop(0, lag, expand)
    loop(lag, nq, expand, lambda q: last(q - lag))
    loop(nq - lag, nq, last)

    wait(vrow.at[:, pl.ds(0, full - tk)], sem_v.at[0])
    wait(vall.at[pl.ds(0, nr - 1)], sem_v.at[2])

    def finish(q):
        wait(put_r.at[0, pl.ds(0, 2 * (near - 1))], f_send.at[q])
        wait(put_l.at[0, pl.ds(0, 2 * (near - 1))], b_send.at[1, q])
        wait(prod.at[0, :, pl.ds(0, near - 1)], p_send.at[q])
        wait(send_l.at[pl.ds(0, qi * (nc - 1) // nc)], e_send.at[q])
        out_copy(q).wait()

    loop(0, nq, finish)


def hand_over(src, dst, held, sem_in, sem_out):
    parts = sem_in.shape[0]
    size = src.shape[0] // parts
    pieces = [pl.ds(n * size, size) for n in range(parts)]
    reads = [pltpu.make_async_copy(src.at[p], held.at[p], sem_in.at[n]) for n, p in enumerate(pieces)]
    writes = [pltpu.make_async_copy(held.at[p], dst.at[p], sem_out.at[n]) for n, p in enumerate(pieces)]
    for read in reads:
        read.start()
    for read, write in zip(reads, writes):
        read.wait()
        write.start()
    for write in writes:
        write.wait()


def solution(mesh):
    nr, nc = mesh.shape["row"], mesh.shape["col"]
    nq = 16

    def on_device(pair_rep, pair_mask, w_left_gate, w_left_proj, w_right_gate, w_right_proj, w_gate, w_out):
        ti, tk, cz = pair_rep.shape
        ch = w_left_gate.shape[1]
        cc, dc = ch // nc, ch // nc // nr
        qi = ti // nq
        tile = pltpu.VMEM((ti, ch, tk), BF)
        sem = pltpu.SemaphoreType.DMA
        update = pl.pallas_call(
            functools.partial(kernel, nr, nc, nq),
            out_shape=jax.ShapeDtypeStruct(pair_rep.shape, pair_rep.dtype),
            in_specs=[pl.BlockSpec(memory_space=pl.ANY)] * 8,
            out_specs=pl.BlockSpec(memory_space=pl.ANY),
            scratch_shapes=[
                tile, tile, tile, tile,
                pltpu.VMEM((ti, cc, nc * tk), BF), pltpu.VMEM((ti, cc, nc * tk), BF),
                pltpu.VMEM((nq, nr, dc * qi, VALID), BF), pltpu.VMEM((nq, nr, dc * qi, VALID), BF),
                pltpu.VMEM((2, nr, nq, dc * qi, VALID), BF), pltpu.VMEM((nq, 2, nr // 2, dc * qi, VALID), BF),
                pltpu.VMEM((2, dc, VALID, VALID), BF),
                pltpu.VMEM((nq, 2, nr // 2, dc * qi, VALID), BF),
                pltpu.VMEM((nq, nr, dc * qi, VALID), BF),
                pltpu.VMEM((VALID, nc * tk), BF),
                pltpu.VMEM((6, ch, cz), BF), pltpu.VMEM((6, ch, cz), BF),
                pltpu.VMEM((ti, tk), jnp.int32), pltpu.VMEM((ti, tk), F32), pltpu.VMEM((8, tk), F32),
                pltpu.VMEM((8, nc * tk), F32), pltpu.VMEM((nc, tk), F32), pltpu.VMEM((nr, nc, tk), F32),
                pltpu.VMEM((2, qi * cc, qi * cc), BF), pltpu.VMEM((ch, ch), BF),
                sem((7,)), sem((nq,)), sem((nq,)), sem((4,)), sem((2, nq)), sem((2, nq)), sem((2, nq)),
                sem((nq,)), sem((nq,)), sem(()), sem((nq,)), sem((nq,)), sem((nq,)), sem((nq,)), sem((nq,)),
            ],
            compiler_params=pltpu.CompilerParams(
                collective_id=0, has_side_effects=True, vmem_limit_bytes=58 << 20
            ),
        )(pair_rep, pair_mask, w_left_gate, w_left_proj, w_right_gate, w_right_proj, w_gate, w_out)
        return pl.pallas_call(
            hand_over,
            out_shape=jax.ShapeDtypeStruct(pair_rep.shape, pair_rep.dtype),
            in_specs=[pl.BlockSpec(memory_space=pl.ANY)],
            out_specs=pl.BlockSpec(memory_space=pl.ANY),
            scratch_shapes=[pltpu.VMEM(pair_rep.shape, pair_rep.dtype), sem((8,)), sem((8,))],
            compiler_params=pltpu.CompilerParams(vmem_limit_bytes=56 << 20),
        )(update)

    in_specs = (P(("dp", "row"), "col", None), P(("dp", "row"), "col")) + (P(),) * 6
    return jax.shard_map(
        on_device, mesh=mesh, in_specs=in_specs, out_specs=P(("dp", "row"), "col", None), check_vma=False
    )
```

```python
import functools

import jax
import jax.numpy as jnp
from jax import lax
from jax.experimental import pallas as pl
from jax.experimental.pallas import tpu as pltpu
from jax.sharding import PartitionSpec as P

MESH = pl.DeviceIdType.MESH
EPS = 1e-05
VALID = 768
BF = jnp.bfloat16
F32 = jnp.float32


def dot(a, b):
    return jnp.dot(a, b, preferred_element_type=F32)


def dot_t(a, b):
    return lax.dot_general(a, b, (((1,), (1,)), ((), ())), preferred_element_type=F32)


def sigmoid(v):
    return 0.5 * jnp.tanh(0.5 * v) + 0.5


def normalize(v):
    centre = v - jnp.mean(v, axis=0, keepdims=True)
    spread = jnp.mean(centre * centre, axis=0, keepdims=True)
    return centre * lax.rsqrt(spread + EPS)


def wait(ref, sem):
    pltpu.make_async_copy(ref, ref, sem).wait()


def kernel(
    nr, nc, nq,
    x_hbm, mask_hbm, wlg_hbm, wlp_hbm, wrg_hbm, wrp_hbm, wg_hbm, wo_hbm,
    out_hbm,
    field, normed, send_r, send_l, recv_r, recv_l, put_r, put_l, got_r, got_l,
    packed_r, prod, back, pick, w_in, w_t, mask_in, maskf, vmine, vrow, vpack, vall, perm, eye,
    sem_in, sem_x, sem_out, sem_v, a_send, a_recv, b_send, br_recv, f_send, f_recv, bl_recv, p_send, p_recv, e_send, e_recv,
):
    row = lax.axis_index("row")
    col = lax.axis_index("col")
    ti, tk = mask_in.shape
    ch = w_t.shape[1]
    cc = ch // nc
    dc = cc // nr
    qi = ti // nq
    full = nc * tk
    near = nr // 2
    far_first = sorted(range(1, nc), key=lambda d: -min(d % (nc // 2), -d % (nc // 2)))
    ahead = nq // 4
    behind = nq // 2
    lag = 2
    group = 8

    def col_peer(d):
        return lax.rem(col + d, nc)

    def row_peer(d):
        return lax.rem(row + d + nr, nr)

    def x_copy(q):
        part = pl.ds(pl.multiple_of(q * qi, qi), qi)
        return pltpu.make_async_copy(x_hbm.at[part], field.at[part], sem_x.at[q])

    def out_copy(q):
        part = pl.ds(pl.multiple_of(q * qi, qi), qi)
        return pltpu.make_async_copy(send_r.at[part], out_hbm.at[part], sem_out.at[q])

    barrier = pltpu.get_barrier_semaphore()
    for d in range(1, nc):
        pl.semaphore_signal(barrier, inc=1, device_id={"col": col_peer(d)}, device_id_type=MESH)
    for d in range(1, nr):
        pl.semaphore_signal(barrier, inc=1, device_id={"row": row_peer(d)}, device_id_type=MESH)

    weights = (wrg_hbm, wrp_hbm, wlg_hbm, wlp_hbm, wg_hbm, wo_hbm)
    w_copy = [pltpu.make_async_copy(ref, w_in.at[n], sem_in.at[n]) for n, ref in enumerate(weights)]
    mask_copy = pltpu.make_async_copy(mask_hbm, mask_in, sem_in.at[len(weights)])
    x_copy(0).start()
    for copy in w_copy[:2] + [mask_copy] + w_copy[2:]:
        copy.start()
    for q in range(1, nq):
        x_copy(q).start()

    def turn(n):
        w_copy[n].wait()
        w_t[n] = dot_t(eye[...], w_in[n]).astype(BF)

    eye[...] = (
        lax.broadcasted_iota(jnp.int32, (ch, ch), 0) == lax.broadcasted_iota(jnp.int32, (ch, ch), 1)
    ).astype(F32).astype(BF)
    turn(0)
    turn(1)
    mask_copy.wait()
    maskf[...] = mask_in[...].astype(F32)
    vmine[...] = jnp.broadcast_to(jnp.max(maskf[...], axis=0, keepdims=True), vmine.shape)

    mine = pl.ds(pl.multiple_of(col * tk, tk), tk)

    def lanes(ref, i):
        return jnp.concatenate([ref[i + g] for g in range(group)], axis=1)

    def edges(n, vals, i, dst):
        g = dot(w_t[n], vals)
        p = dot(w_t[n + 1], vals)
        m = jnp.concatenate([maskf[pl.ds(i + h, 1), :] for h in range(group)], axis=1)
        e = (sigmoid(g) * p * m).astype(BF)
        for h in range(group):
            dst[i + h] = e[:, h * tk:(h + 1) * tk]

    def compute_r(q):
        def body(t, carry):
            i = q * qi + t * group
            x = field[pl.ds(i, group)].reshape(group * tk, ch)
            vals = normalize(dot_t(eye[...], x)).astype(BF)
            for h in range(group):
                normed[i + h] = vals[:, h * tk:(h + 1) * tk]
            edges(0, vals, i, send_r)
            return carry

        lax.fori_loop(0, qi // group, body, 0)

    def compute_l(q):
        def body(t, carry):
            i = q * qi + t * group
            edges(2, lanes(normed, i), i, send_l)
            return carry

        lax.fori_loop(0, qi // group, body, 0)

    def start_a(n, q, src, dst):
        part = pl.ds(pl.multiple_of(q * qi, qi), qi)
        for d in far_first:
            to = col_peer(d)
            pltpu.make_async_remote_copy(
                src.at[part, pl.ds(pl.multiple_of(to * cc, cc), cc), :], dst.at[part, :, mine],
                a_send.at[n, q], a_recv.at[n, q],
                device_id={"col": to}, device_id_type=MESH,
            ).start()
        pltpu.make_async_copy(
            src.at[part, pl.ds(pl.multiple_of(col * cc, cc), cc), :], dst.at[part, :, mine],
            a_recv.at[n, q],
        ).start()

    def compact(n, q, src, dst):
        part = pl.ds(pl.multiple_of(q * qi, qi), qi)
        wait(src.at[part], a_recv.at[n, q])

        a = src[part].reshape(qi * cc, full)
        b = dot(perm[0], dot_t(a, pick[...]).astype(BF)).astype(BF)
        dst[q] = b.reshape(nr, dc * qi, VALID)

    def start_near(piece, send, recv):
        for b in range(near - 1, 0, -1):
            for slot_at, d in ((0, b), (1, -b)):
                src, dst = piece(slot_at, b)
                pltpu.make_async_remote_copy(
                    src, dst, send, recv, device_id={"row": row_peer(d)}, device_id_type=MESH
                ).start()

    def ring(r):
        return lax.rem(r + nr, nr)

    def send_right(q):
        def piece(slot, b):
            group_at = row + b if slot == 0 else row - b - 1
            return put_r.at[q, ring(group_at)], got_r.at[slot, row, q]

        start_near(piece, b_send.at[0, q], br_recv.at[q])
        for slot in range(2):
            src = put_r.at[q, ring(row - slot)]
            pltpu.make_async_remote_copy(
                src, got_r.at[1 - slot, row, q], b_send.at[0, q], f_recv,
                device_id={"row": row_peer(1 - 2 * slot)}, device_id_type=MESH,
            ).start()
            pltpu.make_async_copy(src, got_r.at[slot, row, q], f_recv).start()

    def forward_right(q):
        wait(put_r.at[0, pl.ds(0, 2 * (near - 1))], br_recv.at[q])
        for b in range(1, near):
            for slot in range(2):
                r = ring(row - b if slot == 0 else row + b)
                pltpu.make_async_remote_copy(
                    got_r.at[slot, r, q], got_r.at[1 - slot, r, q], f_send.at[q], f_recv,
                    device_id={"row": row_peer(1 - 2 * slot)}, device_id_type=MESH,
                ).start()

    def send_left(q):
        def piece(slot, b):
            group_at = row + b if slot == 0 else row - b - 1
            return put_l.at[q, ring(group_at)], got_l.at[q, slot, b]

        start_near(piece, b_send.at[1, q], bl_recv.at[q])
        for slot in range(2):
            pltpu.make_async_copy(
                put_l.at[q, ring(row - slot)], got_l.at[q, slot, 0], bl_recv.at[q]
            ).start()

    def send_product(q):
        for b in range(near - 1, -1, -1):
            for slot in range(2):
                src = prod.at[q, slot, b]
                dst = back.at[q, ring(row - slot)]
                if b == 0:
                    pltpu.make_async_copy(src, dst, p_recv.at[q]).start()
                else:
                    pltpu.make_async_remote_copy(
                        src, dst, p_send.at[q], p_recv.at[q],
                        device_id={"row": row_peer(-b if slot == 0 else b)}, device_id_type=MESH,
                    ).start()

    def ranks(v):
        a = lax.broadcasted_iota(jnp.int32, (tk, tk), 0)
        b = lax.broadcasted_iota(jnp.int32, (tk, tk), 1)
        upto = (a <= b).astype(F32).astype(BF)
        ones = jnp.ones((tk, tk), BF)
        base = jnp.zeros((v.shape[0], tk), F32)
        out = []
        for n in range(nc):
            block = v[:, n * tk:(n + 1) * tk]
            block16 = block.astype(BF)
            rank = dot(block16, upto) + base - 1.0
            out.append(jnp.where(block > 0.5, rank, -1.0))
            base = base + dot(block16, ones)
        return jnp.concatenate(out, axis=1)

    def fill_pick(v):
        rank = ranks(v)[0:1, :].astype(jnp.int32)

        def body(t, carry):
            p = pl.multiple_of(t * 16, 16)
            place = lax.broadcasted_iota(jnp.int32, (16, full), 0) + p
            pick[pl.ds(p, 16), :] = (place == rank).astype(F32).astype(BF)
            return carry

        lax.fori_loop(0, VALID // 16, body, 0)

    x_copy(0).wait()
    compute_r(0)
    pl.semaphore_wait(barrier, nc - 1 + nr - 1)
    for d in range(1, nc):
        pltpu.make_async_remote_copy(
            vmine, vrow.at[:, mine], sem_v.at[0], sem_v.at[1],
            device_id={"col": col_peer(d)}, device_id_type=MESH,
        ).start()
    pltpu.make_async_copy(vmine, vrow.at[:, mine], sem_v.at[1]).start()

    start_a(0, 0, send_r, recv_r)

    for n in range(2, len(weights)):
        turn(n)
    at = lax.broadcasted_iota(jnp.int32, (cc * qi, cc * qi), 0)
    of = lax.broadcasted_iota(jnp.int32, (cc * qi, cc * qi), 1)
    perm[0] = (of == (at % qi) * cc + at // qi).astype(F32).astype(BF)
    perm[1] = (at == (of % qi) * cc + of // qi).astype(F32).astype(BF)

    def next_r(q):
        x_copy(q).wait()
        compute_r(q)
        start_a(0, q, send_r, recv_r)

    def next_l(q):
        compute_l(q)
        start_a(1, q, send_l, recv_l)

    def loop(low, high, *steps):
        def body(q, carry):
            for step in steps:
                step(q)
            return carry

        lax.fori_loop(low, high, body, 0)

    loop(1, ahead, next_r)

    wait(vrow, sem_v.at[1])
    for n in range(nc):
        vpack[n:n + 1, :] = vrow[0:1, n * tk:(n + 1) * tk]
    for d in range(1, nr):
        pltpu.make_async_remote_copy(
            vpack, vall.at[row], sem_v.at[2], sem_v.at[3],
            device_id={"row": row_peer(d)}, device_id_type=MESH,
        ).start()
    pltpu.make_async_copy(vpack, vall.at[row], sem_v.at[3]).start()
    fill_pick(vrow[...])

    def across_r(q):
        compact(0, q, recv_r, put_r)
        send_right(q)

    def across_l(q):
        compact(1, q, recv_l, put_l)
        send_left(q)

    edge = nq - ahead
    loop(0, behind, across_r, lambda q: next_r(q + ahead))
    loop(behind, edge, across_r, lambda q: next_r(q + ahead), lambda q: forward_right(q - behind))
    loop(edge, nq, across_r, lambda q: next_l(q - edge), lambda q: forward_right(q - behind))
    loop(0, nq - behind, across_l, lambda q: next_l(q + ahead), lambda q: forward_right(q + behind))
    loop(nq - behind, edge, across_l, lambda q: next_l(q + ahead))
    loop(edge, nq, across_l)

    wait(vall, sem_v.at[3])
    valid = jnp.max(vall[...], axis=0)
    fill_pick(jnp.concatenate([jnp.broadcast_to(valid[n:n + 1, :], vmine.shape) for n in range(nc)], axis=1))
    wait(got_r.at[:, pl.ds(0, nr - near + 1)], f_recv)
    loop(0, nq, lambda q: wait(put_r.at[0], b_send.at[0, q]))

    blocks = nq // dc
    for slot in range(2):

        def split(r):
            rows = got_r[slot, r].astype(F32).reshape(nq, dc, qi, VALID)
            for n in range(dc):
                put_r[n * blocks + r] = rows[:, n].reshape(ti, VALID).astype(BF).reshape(nr, dc * qi, VALID)

        def pack(t):
            p = pl.multiple_of(t * 256, 256)
            for n in range(dc):
                rows = put_r[n * blocks:(n + 1) * blocks].reshape(nr * ti, VALID)
                packed_r[slot, n, pl.ds(p, 256), :] = dot(pick[pl.ds(p, 256), :], rows).astype(BF)

        loop(0, nr, split)
        loop(0, VALID // 256, pack)

    which = lax.broadcasted_iota(jnp.int32, (near * dc * qi, VALID), 0) // qi % dc

    def product(q):
        wait(got_l.at[q], bl_recv.at[q])
        for slot in range(2):
            rows = got_l[q, slot].reshape(near * dc * qi, VALID)
            out = dot_t(rows, packed_r[slot, 0])
            for n in range(1, dc):
                out = jnp.where(which == n, dot_t(rows, packed_r[slot, n]), out)
            prod[q, slot] = out.astype(BF).reshape(near, dc * qi, VALID)
        send_product(q)

    loop(0, nq, product)

    def expand(q):
        part = pl.ds(pl.multiple_of(q * qi, qi), qi)
        wait(send_l.at[pl.ds(0, qi * (nc - 1) // nc)], a_send.at[1, q])
        wait(send_r.at[pl.ds(0, qi * (nc - 1) // nc)], a_send.at[0, q])
        wait(back.at[q], p_recv.at[q])

        a = back[q].reshape(cc * qi, VALID)
        e = dot(dot(perm[1], a).astype(BF), pick[...]).astype(BF)
        for n in range(nc):
            send_l[part, n * cc:(n + 1) * cc, :] = e[:, n * tk:(n + 1) * tk].reshape(qi, cc, tk)
        dst = field.at[part, pl.ds(pl.multiple_of(col * cc, cc), cc), :]
        for d in far_first:
            to = col_peer(d)
            pltpu.make_async_remote_copy(
                send_l.at[part, pl.ds(pl.multiple_of(to * cc, cc), cc), :], dst,
                e_send.at[q], e_recv.at[q],
                device_id={"col": to}, device_id_type=MESH,
            ).start()
        pltpu.make_async_copy(
            send_l.at[part, pl.ds(pl.multiple_of(col * cc, cc), cc), :], dst, e_recv.at[q]
        ).start()

    def last(q):
        part = pl.ds(pl.multiple_of(q * qi, qi), qi)
        wait(field.at[part], e_recv.at[q])

        def body(t, carry):
            i = q * qi + t * group
            mixed = normalize(lanes(field, i).astype(F32)).astype(BF)
            u = (sigmoid(dot(w_t[4], lanes(normed, i))) * dot(w_t[5], mixed)).astype(BF)
            for h in range(group):
                send_r[i + h] = dot_t(eye[...], u[:, h * tk:(h + 1) * tk]).astype(BF)
            return carry

        lax.fori_loop(0, qi // group, body, 0)
        out_copy(q).start()

    loop(0, lag, expand)
    loop(lag, nq, expand, lambda q: last(q - lag))
    loop(nq - lag, nq, last)

    wait(vrow.at[:, pl.ds(0, full - tk)], sem_v.at[0])
    wait(vall.at[pl.ds(0, nr - 1)], sem_v.at[2])

    def finish(q):
        wait(put_r.at[0, pl.ds(0, 2 * (near - 1))], f_send.at[q])
        wait(put_l.at[0, pl.ds(0, 2 * (near - 1))], b_send.at[1, q])
        wait(prod.at[0, :, pl.ds(0, near - 1)], p_send.at[q])
        wait(send_l.at[pl.ds(0, qi * (nc - 1) // nc)], e_send.at[q])
        out_copy(q).wait()

    loop(0, nq, finish)


def hand_over(src, dst, held, sem_in, sem_out):
    parts = sem_in.shape[0]
    size = src.shape[0] // parts
    pieces = [pl.ds(n * size, size) for n in range(parts)]
    reads = [pltpu.make_async_copy(src.at[p], held.at[p], sem_in.at[n]) for n, p in enumerate(pieces)]
    writes = [pltpu.make_async_copy(held.at[p], dst.at[p], sem_out.at[n]) for n, p in enumerate(pieces)]
    for read in reads:
        read.start()
    for read, write in zip(reads, writes):
        read.wait()
        write.start()
    for write in writes:
        write.wait()


def solution(mesh):
    nr, nc = mesh.shape["row"], mesh.shape["col"]
    nq = 16

    def on_device(pair_rep, pair_mask, w_left_gate, w_left_proj, w_right_gate, w_right_proj, w_gate, w_out):
        ti, tk, cz = pair_rep.shape
        ch = w_left_gate.shape[1]
        cc, dc = ch // nc, ch // nc // nr
        qi = ti // nq
        tile = pltpu.VMEM((ti, ch, tk), BF)
        sem = pltpu.SemaphoreType.DMA
        update = pl.pallas_call(
            functools.partial(kernel, nr, nc, nq),
            out_shape=jax.ShapeDtypeStruct(pair_rep.shape, pair_rep.dtype),
            in_specs=[pl.BlockSpec(memory_space=pl.ANY)] * 8,
            out_specs=pl.BlockSpec(memory_space=pl.ANY),
            scratch_shapes=[
                tile, tile, tile, tile,
                pltpu.VMEM((ti, cc, nc * tk), BF), pltpu.VMEM((ti, cc, nc * tk), BF),
                pltpu.VMEM((nq, nr, dc * qi, VALID), BF), pltpu.VMEM((nq, nr, dc * qi, VALID), BF),
                pltpu.VMEM((2, nr, nq, dc * qi, VALID), BF), pltpu.VMEM((nq, 2, nr // 2, dc * qi, VALID), BF),
                pltpu.VMEM((2, dc, VALID, VALID), BF),
                pltpu.VMEM((nq, 2, nr // 2, dc * qi, VALID), BF),
                pltpu.VMEM((nq, nr, dc * qi, VALID), BF),
                pltpu.VMEM((VALID, nc * tk), BF),
                pltpu.VMEM((6, ch, cz), BF), pltpu.VMEM((6, ch, cz), BF),
                pltpu.VMEM((ti, tk), jnp.int32), pltpu.VMEM((ti, tk), F32), pltpu.VMEM((8, tk), F32),
                pltpu.VMEM((8, nc * tk), F32), pltpu.VMEM((nc, tk), F32), pltpu.VMEM((nr, nc, tk), F32),
                pltpu.VMEM((2, qi * cc, qi * cc), BF), pltpu.VMEM((ch, ch), BF),
                sem((7,)), sem((nq,)), sem((nq,)), sem((4,)), sem((2, nq)), sem((2, nq)), sem((2, nq)),
                sem((nq,)), sem((nq,)), sem(()), sem((nq,)), sem((nq,)), sem((nq,)), sem((nq,)), sem((nq,)),
            ],
            compiler_params=pltpu.CompilerParams(
                collective_id=0, has_side_effects=True, vmem_limit_bytes=58 << 20
            ),
        )(pair_rep, pair_mask, w_left_gate, w_left_proj, w_right_gate, w_right_proj, w_gate, w_out)
        return pl.pallas_call(
            hand_over,
            out_shape=jax.ShapeDtypeStruct(pair_rep.shape, pair_rep.dtype),
            in_specs=[pl.BlockSpec(memory_space=pl.ANY)],
            out_specs=pl.BlockSpec(memory_space=pl.ANY),
            scratch_shapes=[pltpu.VMEM(pair_rep.shape, pair_rep.dtype), sem((8,)), sem((8,))],
            compiler_params=pltpu.CompilerParams(vmem_limit_bytes=56 << 20),
        )(update)

    in_specs = (P(("dp", "row"), "col", None), P(("dp", "row"), "col")) + (P(),) * 6
    return jax.shard_map(
        on_device, mesh=mesh, in_specs=in_specs, out_specs=P(("dp", "row"), "col", None), check_vma=False
    )
```

```python
import functools

import jax
import jax.numpy as jnp
from jax import lax
from jax.experimental import pallas as pl
from jax.experimental.pallas import tpu as pltpu
from jax.sharding import PartitionSpec as P

MESH = pl.DeviceIdType.MESH
EPS = 1e-05
VALID = 768
BF = jnp.bfloat16
F32 = jnp.float32


def dot(a, b):
    return jnp.dot(a, b, preferred_element_type=F32)


def dot_t(a, b):
    return lax.dot_general(a, b, (((1,), (1,)), ((), ())), preferred_element_type=F32)


def sigmoid(v):
    return 0.5 * jnp.tanh(0.5 * v) + 0.5


def normalize(v):
    centre = v - jnp.mean(v, axis=0, keepdims=True)
    spread = jnp.mean(centre * centre, axis=0, keepdims=True)
    return centre * lax.rsqrt(spread + EPS)


def wait(ref, sem):
    pltpu.make_async_copy(ref, ref, sem).wait()


def kernel(
    nr, nc, nq,
    x_hbm, mask_hbm, wlg_hbm, wlp_hbm, wrg_hbm, wrp_hbm, wg_hbm, wo_hbm,
    out_hbm,
    field, normed, send_r, send_l, recv_r, recv_l, put_r, put_l, got_r, got_l,
    packed_r, prod, back, pick, w_in, w_t, mask_in, maskf, vmine, vrow, vpack, vall, perm, eye,
    sem_in, sem_x, sem_out, sem_v, a_send, a_recv, b_send, br_recv, f_send, f_recv, bl_recv, p_send, p_recv, e_send, e_recv,
):
    row = lax.axis_index("row")
    col = lax.axis_index("col")
    ti, tk = mask_in.shape
    ch = w_t.shape[1]
    cc = ch // nc
    dc = cc // nr
    qi = ti // nq
    full = nc * tk
    near = nr // 2
    ahead = nq // 4
    behind = nq // 2
    lag = 2
    group = 8

    def col_peer(d):
        return lax.rem(col + d, nc)

    def row_peer(d):
        return lax.rem(row + d + nr, nr)

    def x_copy(q):
        part = pl.ds(pl.multiple_of(q * qi, qi), qi)
        return pltpu.make_async_copy(x_hbm.at[part], field.at[part], sem_x.at[q])

    def out_copy(q):
        part = pl.ds(pl.multiple_of(q * qi, qi), qi)
        return pltpu.make_async_copy(send_r.at[part], out_hbm.at[part], sem_out.at[q])

    barrier = pltpu.get_barrier_semaphore()
    for d in range(1, nc):
        pl.semaphore_signal(barrier, inc=1, device_id={"col": col_peer(d)}, device_id_type=MESH)
    for d in range(1, nr):
        pl.semaphore_signal(barrier, inc=1, device_id={"row": row_peer(d)}, device_id_type=MESH)

    weights = (wrg_hbm, wrp_hbm, wlg_hbm, wlp_hbm, wg_hbm, wo_hbm)
    w_copy = [pltpu.make_async_copy(ref, w_in.at[n], sem_in.at[n]) for n, ref in enumerate(weights)]
    mask_copy = pltpu.make_async_copy(mask_hbm, mask_in, sem_in.at[len(weights)])
    x_copy(0).start()
    for copy in w_copy[:2] + [mask_copy] + w_copy[2:]:
        copy.start()
    for q in range(1, nq):
        x_copy(q).start()

    def turn(n):
        w_copy[n].wait()
        w_t[n] = dot_t(eye[...], w_in[n]).astype(BF)

    eye[...] = (
        lax.broadcasted_iota(jnp.int32, (ch, ch), 0) == lax.broadcasted_iota(jnp.int32, (ch, ch), 1)
    ).astype(F32).astype(BF)
    turn(0)
    turn(1)
    mask_copy.wait()
    maskf[...] = mask_in[...].astype(F32)
    vmine[...] = jnp.broadcast_to(jnp.max(maskf[...], axis=0, keepdims=True), vmine.shape)

    mine = pl.ds(pl.multiple_of(col * tk, tk), tk)

    def lanes(ref, i):
        return jnp.concatenate([ref[i + g] for g in range(group)], axis=1)

    def edges(n, vals, i, dst):
        g = dot(w_t[n], vals)
        p = dot(w_t[n + 1], vals)
        m = jnp.concatenate([maskf[pl.ds(i + h, 1), :] for h in range(group)], axis=1)
        e = (sigmoid(g) * p * m).astype(BF)
        for h in range(group):
            dst[i + h] = e[:, h * tk:(h + 1) * tk]

    def compute_r(q):
        def body(t, carry):
            i = q * qi + t * group
            x = field[pl.ds(i, group)].reshape(group * tk, ch)
            vals = normalize(dot_t(eye[...], x)).astype(BF)
            for h in range(group):
                normed[i + h] = vals[:, h * tk:(h + 1) * tk]
            edges(0, vals, i, send_r)
            return carry

        lax.fori_loop(0, qi // group, body, 0)

    def compute_l(q):
        def body(t, carry):
            i = q * qi + t * group
            edges(2, lanes(normed, i), i, send_l)
            return carry

        lax.fori_loop(0, qi // group, body, 0)

    def start_a(n, q, src, dst):
        part = pl.ds(pl.multiple_of(q * qi, qi), qi)
        for d in range(1, nc):
            to = col_peer(d)
            pltpu.make_async_remote_copy(
                src.at[part, pl.ds(pl.multiple_of(to * cc, cc), cc), :], dst.at[part, :, mine],
                a_send.at[n, q], a_recv.at[n, q],
                device_id={"col": to}, device_id_type=MESH,
            ).start()
        pltpu.make_async_copy(
            src.at[part, pl.ds(pl.multiple_of(col * cc, cc), cc), :], dst.at[part, :, mine],
            a_recv.at[n, q],
        ).start()

    def compact(n, q, src, dst):
        part = pl.ds(pl.multiple_of(q * qi, qi), qi)
        wait(src.at[part], a_recv.at[n, q])

        a = src[part].reshape(qi * cc, full)
        b = dot(perm[0], dot_t(a, pick[...]).astype(BF)).astype(BF)
        dst[q] = b.reshape(nr, dc * qi, VALID)

    def start_near(piece, send, recv):
        for b in range(1, near):
            for slot_at, d in ((0, b), (1, -b)):
                src, dst = piece(slot_at, b)
                pltpu.make_async_remote_copy(
                    src, dst, send, recv, device_id={"row": row_peer(d)}, device_id_type=MESH
                ).start()

    def ring(r):
        return lax.rem(r + nr, nr)

    def send_right(q):
        def piece(slot, b):
            group_at = row + b if slot == 0 else row - b - 1
            return put_r.at[q, ring(group_at)], got_r.at[slot, row, q]

        start_near(piece, b_send.at[0, q], br_recv.at[q])
        for slot in range(2):
            src = put_r.at[q, ring(row - slot)]
            pltpu.make_async_remote_copy(
                src, got_r.at[1 - slot, row, q], b_send.at[0, q], f_recv,
                device_id={"row": row_peer(1 - 2 * slot)}, device_id_type=MESH,
            ).start()
            pltpu.make_async_copy(src, got_r.at[slot, row, q], f_recv).start()

    def forward_right(q):
        wait(put_r.at[0, pl.ds(0, 2 * (near - 1))], br_recv.at[q])
        for b in range(1, near):
            for slot in range(2):
                r = ring(row - b if slot == 0 else row + b)
                pltpu.make_async_remote_copy(
                    got_r.at[slot, r, q], got_r.at[1 - slot, r, q], f_send.at[q], f_recv,
                    device_id={"row": row_peer(1 - 2 * slot)}, device_id_type=MESH,
                ).start()

    def send_left(q):
        def piece(slot, b):
            group_at = row + b if slot == 0 else row - b - 1
            return put_l.at[q, ring(group_at)], got_l.at[q, slot, b]

        start_near(piece, b_send.at[1, q], bl_recv.at[q])
        for slot in range(2):
            pltpu.make_async_copy(
                put_l.at[q, ring(row - slot)], got_l.at[q, slot, 0], bl_recv.at[q]
            ).start()

    def send_product(q):
        for b in range(near):
            for slot in range(2):
                src = prod.at[q, slot, b]
                dst = back.at[q, ring(row - slot)]
                if b == 0:
                    pltpu.make_async_copy(src, dst, p_recv.at[q]).start()
                else:
                    pltpu.make_async_remote_copy(
                        src, dst, p_send.at[q], p_recv.at[q],
                        device_id={"row": row_peer(-b if slot == 0 else b)}, device_id_type=MESH,
                    ).start()

    def ranks(v):
        a = lax.broadcasted_iota(jnp.int32, (tk, tk), 0)
        b = lax.broadcasted_iota(jnp.int32, (tk, tk), 1)
        upto = (a <= b).astype(F32).astype(BF)
        ones = jnp.ones((tk, tk), BF)
        base = jnp.zeros((v.shape[0], tk), F32)
        out = []
        for n in range(nc):
            block = v[:, n * tk:(n + 1) * tk]
            block16 = block.astype(BF)
            rank = dot(block16, upto) + base - 1.0
            out.append(jnp.where(block > 0.5, rank, -1.0))
            base = base + dot(block16, ones)
        return jnp.concatenate(out, axis=1)

    def fill_pick(v):
        rank = ranks(v)[0:1, :].astype(jnp.int32)

        def body(t, carry):
            p = pl.multiple_of(t * 16, 16)
            place = lax.broadcasted_iota(jnp.int32, (16, full), 0) + p
            pick[pl.ds(p, 16), :] = (place == rank).astype(F32).astype(BF)
            return carry

        lax.fori_loop(0, VALID // 16, body, 0)

    x_copy(0).wait()
    compute_r(0)
    pl.semaphore_wait(barrier, nc - 1 + nr - 1)
    for d in range(1, nc):
        pltpu.make_async_remote_copy(
            vmine, vrow.at[:, mine], sem_v.at[0], sem_v.at[1],
            device_id={"col": col_peer(d)}, device_id_type=MESH,
        ).start()
    pltpu.make_async_copy(vmine, vrow.at[:, mine], sem_v.at[1]).start()

    start_a(0, 0, send_r, recv_r)

    for n in range(2, len(weights)):
        turn(n)
    at = lax.broadcasted_iota(jnp.int32, (cc * qi, cc * qi), 0)
    of = lax.broadcasted_iota(jnp.int32, (cc * qi, cc * qi), 1)
    perm[0] = (of == (at % qi) * cc + at // qi).astype(F32).astype(BF)
    perm[1] = (at == (of % qi) * cc + of // qi).astype(F32).astype(BF)

    def next_r(q):
        x_copy(q).wait()
        compute_r(q)
        start_a(0, q, send_r, recv_r)

    def next_l(q):
        compute_l(q)
        start_a(1, q, send_l, recv_l)

    def loop(low, high, *steps):
        def body(q, carry):
            for step in steps:
                step(q)
            return carry

        lax.fori_loop(low, high, body, 0)

    loop(1, ahead, next_r)

    wait(vrow, sem_v.at[1])
    for n in range(nc):
        vpack[n:n + 1, :] = vrow[0:1, n * tk:(n + 1) * tk]
    for d in range(1, nr):
        pltpu.make_async_remote_copy(
            vpack, vall.at[row], sem_v.at[2], sem_v.at[3],
            device_id={"row": row_peer(d)}, device_id_type=MESH,
        ).start()
    pltpu.make_async_copy(vpack, vall.at[row], sem_v.at[3]).start()
    fill_pick(vrow[...])

    def across_r(q):
        compact(0, q, recv_r, put_r)
        send_right(q)

    def across_l(q):
        compact(1, q, recv_l, put_l)
        send_left(q)

    edge = nq - ahead
    loop(0, behind, across_r, lambda q: next_r(q + ahead))
    loop(behind, edge, across_r, lambda q: next_r(q + ahead), lambda q: forward_right(q - behind))
    loop(edge, nq, across_r, lambda q: next_l(q - edge), lambda q: forward_right(q - behind))
    loop(0, nq - behind, across_l, lambda q: next_l(q + ahead), lambda q: forward_right(q + behind))
    loop(nq - behind, edge, across_l, lambda q: next_l(q + ahead))
    loop(edge, nq, across_l)

    wait(vall, sem_v.at[3])
    valid = jnp.max(vall[...], axis=0)
    fill_pick(jnp.concatenate([jnp.broadcast_to(valid[n:n + 1, :], vmine.shape) for n in range(nc)], axis=1))
    wait(got_r.at[:, pl.ds(0, nr - near + 1)], f_recv)
    loop(0, nq, lambda q: wait(put_r.at[0], b_send.at[0, q]))

    blocks = nq // dc
    for slot in range(2):

        def split(r):
            rows = got_r[slot, r].astype(F32).reshape(nq, dc, qi, VALID)
            for n in range(dc):
                put_r[n * blocks + r] = rows[:, n].reshape(ti, VALID).astype(BF).reshape(nr, dc * qi, VALID)

        def pack(t):
            p = pl.multiple_of(t * 256, 256)
            for n in range(dc):
                rows = put_r[n * blocks:(n + 1) * blocks].reshape(nr * ti, VALID)
                packed_r[slot, n, pl.ds(p, 256), :] = dot(pick[pl.ds(p, 256), :], rows).astype(BF)

        loop(0, nr, split)
        loop(0, VALID // 256, pack)

    which = lax.broadcasted_iota(jnp.int32, (near * dc * qi, VALID), 0) // qi % dc

    def product(q):
        wait(got_l.at[q], bl_recv.at[q])
        for slot in range(2):
            rows = got_l[q, slot].reshape(near * dc * qi, VALID)
            out = dot_t(rows, packed_r[slot, 0])
            for n in range(1, dc):
                out = jnp.where(which == n, dot_t(rows, packed_r[slot, n]), out)
            prod[q, slot] = out.astype(BF).reshape(near, dc * qi, VALID)
        send_product(q)

    loop(0, nq, product)

    def expand(q):
        part = pl.ds(pl.multiple_of(q * qi, qi), qi)
        wait(send_l.at[pl.ds(0, qi * (nc - 1) // nc)], a_send.at[1, q])
        wait(send_r.at[pl.ds(0, qi * (nc - 1) // nc)], a_send.at[0, q])
        wait(back.at[q], p_recv.at[q])

        a = back[q].reshape(cc * qi, VALID)
        e = dot(dot(perm[1], a).astype(BF), pick[...]).astype(BF)
        for n in range(nc):
            send_l[part, n * cc:(n + 1) * cc, :] = e[:, n * tk:(n + 1) * tk].reshape(qi, cc, tk)
        dst = field.at[part, pl.ds(pl.multiple_of(col * cc, cc), cc), :]
        for d in range(1, nc):
            to = col_peer(d)
            pltpu.make_async_remote_copy(
                send_l.at[part, pl.ds(pl.multiple_of(to * cc, cc), cc), :], dst,
                e_send.at[q], e_recv.at[q],
                device_id={"col": to}, device_id_type=MESH,
            ).start()
        pltpu.make_async_copy(
            send_l.at[part, pl.ds(pl.multiple_of(col * cc, cc), cc), :], dst, e_recv.at[q]
        ).start()

    def last(q):
        part = pl.ds(pl.multiple_of(q * qi, qi), qi)
        wait(field.at[part], e_recv.at[q])

        def body(t, carry):
            i = q * qi + t * group
            mixed = normalize(lanes(field, i).astype(F32)).astype(BF)
            u = (sigmoid(dot(w_t[4], lanes(normed, i))) * dot(w_t[5], mixed)).astype(BF)
            for h in range(group):
                send_r[i + h] = dot_t(eye[...], u[:, h * tk:(h + 1) * tk]).astype(BF)
            return carry

        lax.fori_loop(0, qi // group, body, 0)
        out_copy(q).start()

    loop(0, lag, expand)
    loop(lag, nq, expand, lambda q: last(q - lag))
    loop(nq - lag, nq, last)

    wait(vrow.at[:, pl.ds(0, full - tk)], sem_v.at[0])
    wait(vall.at[pl.ds(0, nr - 1)], sem_v.at[2])

    def finish(q):
        wait(put_r.at[0, pl.ds(0, 2 * (near - 1))], f_send.at[q])
        wait(put_l.at[0, pl.ds(0, 2 * (near - 1))], b_send.at[1, q])
        wait(prod.at[0, :, pl.ds(0, near - 1)], p_send.at[q])
        wait(send_l.at[pl.ds(0, qi * (nc - 1) // nc)], e_send.at[q])
        out_copy(q).wait()

    loop(0, nq, finish)


def hand_over(src, dst, held, sem_in, sem_out):
    parts = sem_in.shape[0]
    size = src.shape[0] // parts
    pieces = [pl.ds(n * size, size) for n in range(parts)]
    reads = [pltpu.make_async_copy(src.at[p], held.at[p], sem_in.at[n]) for n, p in enumerate(pieces)]
    writes = [pltpu.make_async_copy(held.at[p], dst.at[p], sem_out.at[n]) for n, p in enumerate(pieces)]
    for read in reads:
        read.start()
    for read, write in zip(reads, writes):
        read.wait()
        write.start()
    for write in writes:
        write.wait()


def solution(mesh):
    nr, nc = mesh.shape["row"], mesh.shape["col"]
    nq = 16

    def on_device(pair_rep, pair_mask, w_left_gate, w_left_proj, w_right_gate, w_right_proj, w_gate, w_out):
        ti, tk, cz = pair_rep.shape
        ch = w_left_gate.shape[1]
        cc, dc = ch // nc, ch // nc // nr
        qi = ti // nq
        tile = pltpu.VMEM((ti, ch, tk), BF)
        sem = pltpu.SemaphoreType.DMA
        update = pl.pallas_call(
            functools.partial(kernel, nr, nc, nq),
            out_shape=jax.ShapeDtypeStruct(pair_rep.shape, pair_rep.dtype),
            in_specs=[pl.BlockSpec(memory_space=pl.ANY)] * 8,
            out_specs=pl.BlockSpec(memory_space=pl.ANY),
            scratch_shapes=[
                tile, tile, tile, tile,
                pltpu.VMEM((ti, cc, nc * tk), BF), pltpu.VMEM((ti, cc, nc * tk), BF),
                pltpu.VMEM((nq, nr, dc * qi, VALID), BF), pltpu.VMEM((nq, nr, dc * qi, VALID), BF),
                pltpu.VMEM((2, nr, nq, dc * qi, VALID), BF), pltpu.VMEM((nq, 2, nr // 2, dc * qi, VALID), BF),
                pltpu.VMEM((2, dc, VALID, VALID), BF),
                pltpu.VMEM((nq, 2, nr // 2, dc * qi, VALID), BF),
                pltpu.VMEM((nq, nr, dc * qi, VALID), BF),
                pltpu.VMEM((VALID, nc * tk), BF),
                pltpu.VMEM((6, ch, cz), BF), pltpu.VMEM((6, ch, cz), BF),
                pltpu.VMEM((ti, tk), jnp.int32), pltpu.VMEM((ti, tk), F32), pltpu.VMEM((8, tk), F32),
                pltpu.VMEM((8, nc * tk), F32), pltpu.VMEM((nc, tk), F32), pltpu.VMEM((nr, nc, tk), F32),
                pltpu.VMEM((2, qi * cc, qi * cc), BF), pltpu.VMEM((ch, ch), BF),
                sem((7,)), sem((nq,)), sem((nq,)), sem((4,)), sem((2, nq)), sem((2, nq)), sem((2, nq)),
                sem((nq,)), sem((nq,)), sem(()), sem((nq,)), sem((nq,)), sem((nq,)), sem((nq,)), sem((nq,)),
            ],
            compiler_params=pltpu.CompilerParams(
                collective_id=0, has_side_effects=True, vmem_limit_bytes=58 << 20
            ),
        )(pair_rep, pair_mask, w_left_gate, w_left_proj, w_right_gate, w_right_proj, w_gate, w_out)
        return pl.pallas_call(
            hand_over,
            out_shape=jax.ShapeDtypeStruct(pair_rep.shape, pair_rep.dtype),
            in_specs=[pl.BlockSpec(memory_space=pl.ANY)],
            out_specs=pl.BlockSpec(memory_space=pl.ANY),
            scratch_shapes=[pltpu.VMEM(pair_rep.shape, pair_rep.dtype), sem((16,)), sem((16,))],
            compiler_params=pltpu.CompilerParams(vmem_limit_bytes=56 << 20),
        )(update)

    in_specs = (P(("dp", "row"), "col", None), P(("dp", "row"), "col")) + (P(),) * 6
    return jax.shard_map(
        on_device, mesh=mesh, in_specs=in_specs, out_specs=P(("dp", "row"), "col", None), check_vma=False
    )
```
